32 devices in a mesh: blk: 8 (over z, core), rep: 4 (over y, x).
Axes of the slice: x: 2, y: 2, z: 4, core: 2. Of those that a mesh axis runs over, the one named last changes fastest.
Arguments:
- t_slab: bfloat16 [4, 1024, 8, 1024], P('rep', 'blk'), may hold values from -12 to 12
- w_cycle: bfloat16 [4, 1, 1024, 1024], P('rep'), may hold values from -0.75 to 0.75
- k_irrep: int32 [4], P('rep'), may hold values from 0 to 7
- i_irrep: int32 [8], replicated, may hold values from 0 to 7, as said below
- j_irrep: int32 [1], replicated, may hold values from 0 to 7
- tile_irrep: int32 [8], replicated, may hold values from 0 to 7, each once
- i_energy: float32 [8], replicated, may hold values from -2.5 to -0.5
- j_energy: float32 [1], replicated, may hold values from -2.5 to -0.5
- vir_energy: float32 [1024], replicated, may hold values from 0.3 to 3
Outputs:
- amplitude_update: float32 [1, 8, 1024, 1024], P(None, None, 'blk', 'rep')
The draws below stay inside these ranges and needn't reach their ends.
Inputs may be any that keep to these rules, and one draw needn't show every extreme that they name: tile_irrep holds each of the 8 irreps exactly once. The orbitals i come in 8 runs of 1 consecutive orbitals; i_irrep is the same within a run, and each irrep labels exactly one run.
All inputs are finite; a program needn't handle non-finite values.
Results may differ from the reference program's by a relative error of at most 0.0003.
Values may be sent and summed in bfloat16 or wider, within the bound.
No kernel may reach another device: no remote copies, remote signals or barrier semaphores. Data moves between devices by JAX's collectives and lax.ppermute only.
A program may use at most 64 MiB of HBM per device.

```python
import jax
import jax.numpy as jnp
from jax import lax

TILE = 128
VP = 1024
NJ = 1
NI = 8
NK = 4


def draw_i_irrep(key, part):
    key = jax.random.fold_in(key, 11)
    order = jax.random.permutation(key, jnp.arange(8, dtype=jnp.int32))
    runs = jnp.arange(NI, dtype=jnp.int32) // (NI // 8)
    return order[runs].astype(jnp.int32)


def with_ends(drawn, stream_key, least, top_value):
    spot = [jax.random.randint(jax.random.fold_in(stream_key, axis), (), 0, length) for axis, length in enumerate(drawn.shape)]
    main_axis = drawn.shape.index(max(drawn.shape))
    neighbour = spot[:main_axis] + [(spot[main_axis] + 1) % drawn.shape[main_axis]] + spot[main_axis + 1:]
    return drawn.at[tuple(spot)].set(least).at[tuple(neighbour)].set(top_value)


def raised(values, key, source, target, blocks, factor):
    def block_of(position):
        return (jnp.arange(values.shape[position]) // (values.shape[position] // blocks)).reshape((-1,) + (1,) * (values.ndim - 1 - position))

    one_side = jax.random.permutation(key, blocks)[block_of(target)]
    second = (block_of(target) + blocks // 2) % blocks
    return jnp.where((block_of(source) == one_side) | (block_of(source) == second), factor * values, values)


def steps_of(own_key, shape, shards, low, high):
    gain = 1.0
    for position, parts in shards:
        heights = jax.random.uniform(jax.random.fold_in(jax.random.fold_in(own_key, 6), position), (parts,), jnp.float32, low / len(shards), high / len(shards))
        gain = gain * jnp.repeat(jnp.exp(heights), shape[position] // parts).reshape((-1,) + (1,) * (len(shape) - 1 - position))
    return gain


def bell_draw(key, shape, deviation, bound, cuts=(), held_as=jnp.bfloat16):
    values = jax.random.normal(key, shape, jnp.float32) * deviation
    if len(cuts) > 0:
        values = steps_of(key, shape, cuts, -0.22, 0.18) * values
    return jnp.clip(values, min=-bound, max=bound).astype(held_as)


def bell_draw_with(own_key, shape, spread, bound, cuts, heavy, held_as=jnp.bfloat16):
    drawn = spread * jax.random.normal(own_key, shape, jnp.float32)
    if cuts:
        drawn = drawn * steps_of(own_key, shape, cuts, -0.22, 0.18)
    return jnp.clip(raised(drawn, jax.random.fold_in(own_key, 3), *heavy), -bound, bound).astype(held_as)


def setup_inputs(seed: int = 0) -> dict:
    streams_of = jax.random.split(jax.random.key(seed), 10)
    return {
        "t_slab": bell_draw(streams_of[0], (NK, VP, NI, VP), 2.0, 12.0, ((0, 4), (1, 8))),
        "w_cycle": bell_draw_with(streams_of[1], (NK, NJ, VP, VP), TILE ** -0.5, 0.75, ((0, 4),), (0, 3, 4, 2.0)),
        "k_irrep": with_ends(jax.random.randint(streams_of[2], (NK,), 0, 8), jax.random.fold_in(streams_of[2], 1), 0, 7).astype(jnp.int32),
        "i_irrep": draw_i_irrep(jax.random.fold_in(streams_of[9], 71), 0),
        "j_irrep": jax.random.randint(streams_of[4], (NJ,), 0, 8).astype(jnp.int32),
        "tile_irrep": jax.random.permutation(streams_of[5], 8).astype(jnp.int32),
        "i_energy": jnp.clip(jax.random.uniform(streams_of[6], (NI,), jnp.float32, -2.5, -0.5), -2.5, -0.5),
        "j_energy": jnp.clip(jax.random.uniform(streams_of[7], (NJ,), jnp.float32, -2.5, -0.5), -2.5, -0.5),
        "vir_energy": jnp.clip(jax.random.uniform(streams_of[8], (VP,), jnp.float32, 0.3, 3.0), 0.3, 3.0),
    }


def reference(t_slab, w_cycle, k_irrep, i_irrep, j_irrep, tile_irrep, i_energy, j_energy, vir_energy):
    vir_irrep = jnp.repeat(tile_irrep, TILE)

    def step(total, pieces):
        amp, cycle_w, k_label = pieces
        mask_amp = jnp.bitwise_xor(jnp.bitwise_xor(k_label, vir_irrep[:, None, None]), jnp.bitwise_xor(i_irrep[None, :, None], vir_irrep[None, None, :])) == 0
        mask_cycle = jnp.bitwise_xor(jnp.bitwise_xor(k_label, j_irrep[:, None, None]), jnp.bitwise_xor(vir_irrep[None, :, None], vir_irrep[None, None, :])) == 0
        left = jnp.where(mask_amp, amp.astype(jnp.float32), jnp.zeros((), jnp.float32))
        right = jnp.where(mask_cycle, cycle_w.astype(jnp.float32), jnp.zeros((), jnp.float32))
        total = total + lax.dot_general(left, right, (((0,), (1,)), ((), ())), precision=lax.Precision.HIGHEST)
        return total, None

    start = jnp.zeros((NI, VP, NJ, VP), jnp.float32)
    cycle, unused = lax.scan(step, start, (t_slab, w_cycle, k_irrep))
    cycle = jnp.transpose(cycle, (2, 0, 1, 3))
    denom = vir_energy[None, None, :, None] + vir_energy[None, None, None, :] - i_energy[None, :, None, None] - j_energy[:, None, None, None]
    return cycle / denom
```

```python
import jax
import jax.numpy as jnp
from jax import lax
from jax.experimental import pallas as pl
from jax.experimental.pallas import tpu as pltpu
from jax.sharding import PartitionSpec as P

TILE = 128
CHUNK = 256
HALVES = 2
POWER = 17
TOP = 128.0
LEAST = 2.0**-100
SMALLEST = 2.0**-126
SPARE = 16


def vmem():
    return pl.BlockSpec(memory_space=pltpu.VMEM)


def hbm():
    return pl.BlockSpec(memory_space=pltpu.HBM)


def small(array):
    return pltpu.SMEM(array.shape, array.dtype)


def limit(mebibytes):
    return pltpu.CompilerParams(vmem_limit_bytes=mebibytes * 2**20)


def place_of(ref, stride, label):
    found = jnp.int32(0)
    for n in range(ref.shape[0] // stride):
        found = jnp.where(ref[n * stride] == label, jnp.int32(n), found)
    return found


def start_all(sources, targets, sems):
    copies = []
    for n, (source, target) in enumerate(zip(sources, targets)):
        copies.append(pltpu.make_async_copy(source, target, sems.at[n]))
        copies[-1].start()
    return copies


def pack_kernel(plan, *refs):
    rows_i, run, c_width, by_partner, tiles_b, groups, steps = plan
    if steps:
        k_hbm, i_hbm, tile_hbm, t_hbm, j_hbm, w_hbm, *refs = refs
        *refs, j_ref, w_sems = refs
    else:
        k_hbm, i_hbm, tile_hbm, t_hbm, *refs = refs
        outs_hbm, refs = refs[: len(groups)], refs[len(groups) :]
        *refs, out_sems = refs
    *refs, k_ref, i_ref, tile_ref, t_ref, small_sems, t_sems = refs
    out_refs = refs[: len(groups)]
    runs = rows_i // run
    rows = CHUNK // runs
    sources, targets = [k_hbm, i_hbm, tile_hbm], [k_ref, i_ref, tile_ref]
    if steps:
        sources.append(j_hbm)
        targets.append(j_ref)
    small_copies = start_all(sources, targets, small_sems)
    me = lax.axis_index("blk") if by_partner else 0
    places = {
        step: (out_ref, spot)
        for out_ref, group in zip(out_refs, groups)
        for spot, step in enumerate(group)
    }
    pairs = [step for step in places if step % 2 == 0]
    columns = [
        pl.ds(pl.multiple_of(((me ^ step) | 1) * TILE - TILE, 2 * TILE), 2 * TILE)
        for step in pairs
    ]
    depth = t_ref.shape[1] // HALVES
    spans = [(n, pl.ds(half * depth, depth)) for n in range(len(pairs)) for half in range(HALVES)]
    t_copies = start_all(
        [t_hbm.at[span, columns[n]] for n, span in spans],
        [t_ref.at[n, span] for n, span in spans],
        t_sems,
    )
    row = lax.broadcasted_iota(jnp.int32, (rows, CHUNK), 0)
    col = lax.broadcasted_iota(jnp.int32, (rows, CHUNK), 1)
    run_bits = run.bit_length() - 1
    same_c = (row >> run_bits) == (col >> (rows_i.bit_length() - 1))
    same_m = (row & (run - 1)) == (col & (run - 1))
    of_run = jnp.where(same_c & same_m, (col >> run_bits) & (runs - 1), -1)
    own_tile = lax.axis_index("blk") * c_width // TILE
    for copy in small_copies:
        copy.wait()
    w_copies = []
    if steps:
        w_ref, choice_ref = refs[len(groups) :]
        side = lax.axis_index("rep") * tiles_b if by_partner else 0
        flip = len(steps) - tiles_b if by_partner else 0
        label_w = k_ref[0] ^ j_ref[0]
        spot_row = lax.broadcasted_iota(jnp.int32, choice_ref.shape[1:], 0)
        for n in range(len(steps)):
            b_tile = n ^ flip ^ side
            c_tile = place_of(tile_ref, 1, label_w ^ tile_ref[b_tile])
            source = w_hbm.at[
                pl.ds(pl.multiple_of(c_tile * TILE, TILE), TILE),
                pl.ds(pl.multiple_of(b_tile * TILE, TILE), TILE),
            ]
            target = w_ref.at[:, pl.ds(n * TILE, TILE)]
            w_copies.append(pltpu.make_async_copy(source, target, w_sems.at[n]))
            w_copies[-1].start()
            spot = jnp.int32(0)
            for where, step in enumerate(steps):
                spot = jnp.where((c_tile ^ me) == step, jnp.int32(where), spot)
            choice_ref[n] = jnp.where(spot_row == spot, 1.0, 0.0)
    label = k_ref[0] ^ tile_ref[own_tile]
    picks = []
    for step in pairs:
        rows_of_pair = []
        for own in (step, step + 1):
            chosen = place_of(i_ref, run, label ^ tile_ref[me ^ own])
            rows_of_pair.append(jnp.where(of_run == chosen, 1.0, 0.0).astype(jnp.bfloat16))
        picks.append(jnp.concatenate(rows_of_pair, axis=0))
    swapped = (me & 1) == 1
    out_copies = []
    for n, step in enumerate(pairs):
        for chunk in range(t_ref.shape[1] // CHUNK):
            if chunk * CHUNK % depth == 0:
                t_copies[n * HALVES + chunk * CHUNK // depth].wait()
            block = t_ref[n, chunk * CHUNK : (chunk + 1) * CHUNK, :]
            kept = jnp.dot(picks[n], block, preferred_element_type=jnp.float32)
            low, high = kept[:, :TILE], kept[:, TILE:]
            for own, here, other in ((step, low, high), (step + 1, high, low)):
                half = slice((own - step) * rows, (own - step + 1) * rows)
                out_ref, spot = places[own]
                value = jnp.where(swapped, other[half], here[half])
                out_ref[spot, chunk * rows : (chunk + 1) * rows, :] = value.astype(out_ref.dtype)
        if not steps:
            out_copies.append(pltpu.make_async_copy(out_ref, outs_hbm[n], out_sems.at[n]))
            out_copies[-1].start()
    for copy in w_copies + out_copies:
        copy.wait()


def write_coded(out_ref, value):
    rows, width = value.shape
    largest = jnp.max(jnp.max(jnp.abs(value), axis=0, keepdims=True), axis=1, keepdims=True)
    exponent = jnp.ceil(jnp.log2(jnp.maximum(largest, LEAST)))
    scaled = value * (TOP * jnp.exp2(-exponent))
    power = scaled
    for _ in range(POWER.bit_length() - 1):
        power = power * power
    out_ref[:rows, :] = (power * scaled).astype(out_ref.dtype)
    out_ref[rows:, :] = jnp.broadcast_to(exponent, (SPARE, width)).astype(out_ref.dtype)


def read_coded(ref):
    rows = ref.shape[0] - SPARE
    power = ref[:rows, :].astype(jnp.float32)
    exponent = ref[rows:, :].astype(jnp.float32)[:1, :]
    size = jnp.exp2(jnp.log2(jnp.maximum(jnp.abs(power), SMALLEST)) * (1.0 / POWER))
    size = jnp.where(power < 0, -size, size) * (jnp.exp2(exponent) * (1.0 / TOP))
    return jnp.where(power == 0, 0.0, size)


def multiply_kernel(spots, out_count, w_ref, choice_ref, *refs):
    out_refs = refs[-out_count:]
    blocks = [refs[n][spot] for n, spot in spots]
    tiles = choice_ref.shape[0]
    each = tiles // out_count
    for n, out_ref in enumerate(out_refs):
        products = []
        for tile in range(n * each, (n + 1) * each):
            left = jnp.zeros_like(blocks[0])
            for spot, block in enumerate(blocks):
                left = jnp.where(choice_ref[tile, spot : spot + 1, :] > 0.5, block, left)
            products.append(
                lax.dot_general(
                    left,
                    w_ref[:, tile * TILE : (tile + 1) * TILE],
                    (((0,), (0,)), ((), ())),
                    preferred_element_type=jnp.float32,
                )
            )
        value = jnp.concatenate(products, axis=1)
        if out_ref.dtype == jnp.float32:
            out_ref[...] = value
        else:
            write_coded(out_ref, value)


def scale_kernel(
    a_width, i_hbm, j_hbm, tile_hbm, ei_hbm, ej_hbm, ev_ref, after_hbm, denom_ref, run_ref,
    zero_hbm, i_ref, j_ref, tile_ref, ei_ref, ej_ref, column_ref, zero_ref, sems, zero_sems,
):
    copies = start_all(
        (i_hbm, j_hbm, tile_hbm, ei_hbm, ej_hbm), (i_ref, j_ref, tile_ref, ei_ref, ej_ref), sems
    )
    rows_i, b_width = i_ref.shape[0], run_ref.shape[1]
    run = rows_i // tile_ref.shape[0]
    zero_ref[...] = jnp.zeros_like(zero_ref)
    count = zero_ref.shape[0]
    zero_copies = start_all(
        [zero_ref] * (rows_i // count),
        [zero_hbm.at[pl.ds(n * count, count)] for n in range(rows_i // count)],
        zero_sems,
    )
    a_start = lax.axis_index("blk") * a_width
    b_start = lax.axis_index("rep") * b_width
    a_tile = a_start // TILE
    column_ref[...] = jnp.broadcast_to(ev_ref[pl.ds(a_tile, 1), :], (TILE, TILE)).T
    a_energy = column_ref[pl.ds(pl.multiple_of(a_start % TILE, a_width), a_width), :]
    width = min(TILE, b_width)
    for copy in copies:
        copy.wait()
    for part in range(b_width // width):
        b_tile = b_start // TILE + part
        b_tile_row = ev_ref[pl.ds(b_tile, 1), :]
        b_row = b_tile_row[:, :width]
        for n in range(1, TILE // width):
            piece = b_tile_row[:, n * width : (n + 1) * width]
            b_row = jnp.where(b_start % TILE == n * width, piece, b_row)
        chosen = place_of(i_ref, run, j_ref[0] ^ tile_ref[a_tile] ^ tile_ref[b_tile])
        columns = slice(part * width, (part + 1) * width)
        run_ref[:, columns] = jnp.full((run_ref.shape[0], width), chosen.astype(jnp.float32))
        sum_ab = a_energy[:, :width] + b_row
        for m in range(run):
            denom_ref[m * a_width : (m + 1) * a_width, columns] = (
                sum_ab - ei_ref[chosen * run + m] - ej_ref[0]
            )
    for copy in zero_copies:
        copy.wait()


def place_kernel(run, denom_ref, run_ref, zero_hbm, *refs):
    parts_refs, out_hbm, block_ref, sems = refs[:-3], refs[-3], refs[-2], refs[-1]
    a_width, width = block_ref.shape[2:]
    total = parts_refs[-1][...]
    for parts_ref in parts_refs[:-1]:
        coded = parts_ref.dtype != jnp.float32
        total = total + (read_coded(parts_ref) if coded else parts_ref[...])
    scaled = total / denom_ref[...]
    copies = []
    for part in range(block_ref.shape[0]):
        columns = slice(part * width, (part + 1) * width)
        chosen = jnp.max(run_ref[:, columns]).astype(jnp.int32)
        for m in range(run):
            block_ref[part, m] = scaled[m * a_width : (m + 1) * a_width, columns]
        target = out_hbm.at[pl.ds(chosen * run, run), :, pl.ds(part * width, width)]
        copies.append(pltpu.make_async_copy(block_ref.at[part], target, sems.at[part]))
        copies[-1].start()
    for copy in copies:
        copy.wait()


def swap(block, axis, step):
    return lax.ppermute(block, axis, [(n, n ^ step) for n in range(lax.axis_size(axis))])


def shards(t_slab, w_cycle, k_irrep, i_irrep, j_irrep, tile_irrep, i_energy, j_energy, vir_energy):
    blk_count = lax.axis_size("blk")
    rep_count = lax.axis_size("rep")
    k_rows, c_width, rows_i, full_width = t_slab.shape
    rows_j = w_cycle.shape[1]
    assert k_rows == 1 and rows_j == 1
    tiles = tile_irrep.shape[0]
    run = rows_i // tiles
    a_width = full_width // blk_count
    b_width = full_width // rep_count
    deep = c_width * run
    wide = run * a_width
    by_partner = a_width == TILE and b_width % TILE == 0
    steps = list(reversed(range(tiles))) if by_partner else list(range(tiles))
    groups = [[step] for step in steps]
    if by_partner:
        far = [4, 6, 2] if tiles == 8 else range(tiles - 2, 0, -2)
        groups = [[step, step + 1] for step in far] + [[1], [0]]
        steps = [step for group in groups for step in group]

    t_rows = t_slab.reshape(c_width * rows_i, full_width)

    def pack(some_groups, last):
        pairs = sum(len(group) for group in some_groups) // 2
        plan = (rows_i, run, c_width, by_partner, b_width // TILE, some_groups, steps * last)
        arguments = [k_irrep, i_irrep, tile_irrep, t_rows]
        shapes = [
            jax.ShapeDtypeStruct((len(group), deep, TILE), t_slab.dtype) for group in some_groups
        ]
        scratch = [
            small(k_irrep),
            small(i_irrep),
            small(tile_irrep),
            pltpu.VMEM((pairs, t_rows.shape[0], 2 * TILE), t_slab.dtype),
            pltpu.SemaphoreType.DMA((3 + last,)),
            pltpu.SemaphoreType.DMA((pairs * HALVES,)),
        ]
        if not last:
            packed_here = [pltpu.VMEM(shape.shape, shape.dtype) for shape in shapes]
            scratch = packed_here + scratch + [pltpu.SemaphoreType.DMA((len(shapes),))]
        if last:
            arguments += [j_irrep, w_cycle.reshape(full_width, full_width)]
            shapes += [
                jax.ShapeDtypeStruct((TILE, full_width), w_cycle.dtype),
                jax.ShapeDtypeStruct((tiles, tiles, TILE), jnp.float32),
            ]
            scratch += [small(j_irrep), pltpu.SemaphoreType.DMA((tiles,))]
        return pl.pallas_call(
            lambda *refs: pack_kernel(plan, *refs),
            in_specs=[hbm()] * len(arguments),
            out_specs=[vmem() if last else hbm()] * len(shapes),
            out_shape=shapes,
            scratch_shapes=scratch,
            compiler_params=limit(52 if last else 62),
            name="pack_near" if last else "pack_far",
        )(*arguments)

    packed = list(pack(groups[:3], False)) if by_partner else []
    *near, chosen_w, choice = pack(groups[len(packed) :], True)
    packed += near

    if by_partner:
        *far, beside, own = packed
        left = [swap(pair, "blk", group[0]) for pair, group in zip(far, groups)]
        left += [swap(beside, "blk", 1), own]
        left[0], left[-2], choice = lax.optimization_barrier((left[0], left[-2], choice))
        handed = [swap(pair, "blk", 1) for pair in left[: len(far)]]
        spots = []
        for n in range(len(far)):
            spots += [(n, 0), (len(left) + n, 1)]
        spots += [(len(far), 0), (len(far) + 1, 0)]
        left += handed
        part_shapes = [
            jax.ShapeDtypeStruct((wide + SPARE, b_width), jnp.bfloat16)
        ] * (rep_count - 1) + [jax.ShapeDtypeStruct((wide, b_width), jnp.float32)]
    else:
        stacked = jnp.concatenate(packed).reshape(tiles, c_width, run, TILE // a_width, a_width)
        outgoing = stacked.transpose(0, 3, 1, 2, 4).reshape(blk_count, c_width, wide)
        arrived = lax.all_to_all(outgoing, "blk", split_axis=0, concat_axis=0, tiled=True)
        left = [arrived.reshape(tiles, TILE, wide)]
        spots = [(0, n) for n in range(tiles)]
        part_shapes = [jax.ShapeDtypeStruct((wide, full_width), jnp.float32)]

    partials = pl.pallas_call(
        lambda *refs: multiply_kernel(spots, len(part_shapes), *refs),
        in_specs=[vmem()] * (2 + len(left)),
        out_specs=[vmem()] * len(part_shapes),
        out_shape=part_shapes,
        compiler_params=limit(16),
        name="multiply",
    )(chosen_w, choice, *left)

    out_shape = jax.ShapeDtypeStruct((rows_i, a_width, b_width), jnp.float32)
    denom, run_row, zeros = pl.pallas_call(
        lambda *refs: scale_kernel(a_width, *refs),
        in_specs=[hbm()] * 5 + [vmem(), pl.BlockSpec(memory_space=pl.ANY)],
        out_specs=[vmem(), vmem(), hbm()],
        out_shape=[
            jax.ShapeDtypeStruct((wide, b_width), jnp.float32),
            jax.ShapeDtypeStruct((8, b_width), jnp.float32),
            out_shape,
        ],
        scratch_shapes=[
            small(i_irrep),
            small(j_irrep),
            small(tile_irrep),
            small(i_energy),
            small(j_energy),
            pltpu.VMEM((TILE, TILE), jnp.float32),
            pltpu.VMEM((run, a_width, b_width), jnp.float32),
            pltpu.SemaphoreType.DMA((5,)),
            pltpu.SemaphoreType.DMA((tiles,)),
        ],
        compiler_params=limit(8),
        name="scale",
    )(
        i_irrep, j_irrep, tile_irrep, i_energy, j_energy,
        vir_energy.reshape(full_width // TILE, TILE), partials[-1],
    )

    if by_partner:
        gathered = [
            swap(part, "rep", rep_count - 1 - n) for n, part in enumerate(partials[:-1])
        ] + [partials[-1]]
    else:
        outgoing = partials[0].reshape(wide, rep_count, b_width).transpose(1, 0, 2)
        arrived = lax.all_to_all(outgoing, "rep", split_axis=0, concat_axis=0, tiled=True)
        gathered = [arrived[n] for n in range(rep_count)]

    part_width = min(TILE, b_width)
    result = pl.pallas_call(
        lambda *refs: place_kernel(run, *refs),
        in_specs=[vmem(), vmem(), hbm()] + [vmem()] * rep_count,
        out_specs=hbm(),
        out_shape=out_shape,
        input_output_aliases={2: 0},
        scratch_shapes=[
            pltpu.VMEM((b_width // part_width, run, a_width, part_width), jnp.float32),
            pltpu.SemaphoreType.DMA((b_width // part_width,)),
        ],
        compiler_params=limit(16),
        name="place",
    )(denom, run_row, zeros, *gathered)
    return result.reshape(rows_j, rows_i, a_width, b_width)


def solution(mesh):
    in_specs = (
        P("rep", "blk", None, None),
        P("rep", None, None, None),
        P("rep"),
        P(),
        P(),
        P(),
        P(),
        P(),
        P(),
    )
    out_specs = P(None, None, "blk", "rep")
    return jax.shard_map(shards, mesh=mesh, in_specs=in_specs, out_specs=out_specs, check_vma=False)
```

```python
import jax
import jax.numpy as jnp
from jax import lax
from jax.experimental import pallas as pl
from jax.experimental.pallas import tpu as pltpu
from jax.sharding import PartitionSpec as P

TILE = 128
CHUNK = 256
POWER = 17
TOP = 128.0
LEAST = 2.0**-100
SMALLEST = 2.0**-126
SPARE = 8


def vmem():
    return pl.BlockSpec(memory_space=pltpu.VMEM)


def hbm():
    return pl.BlockSpec(memory_space=pltpu.HBM)


def small(array):
    return pltpu.SMEM(array.shape, array.dtype)


def limit(mebibytes):
    return pltpu.CompilerParams(vmem_limit_bytes=mebibytes * 2**20)


def place_of(ref, stride, label):
    found = jnp.int32(0)
    for n in range(ref.shape[0] // stride):
        found = jnp.where(ref[n * stride] == label, jnp.int32(n), found)
    return found


def start_all(sources, targets, sems):
    copies = []
    for n, (source, target) in enumerate(zip(sources, targets)):
        copies.append(pltpu.make_async_copy(source, target, sems.at[n]))
        copies[-1].start()
    return copies


def pack_kernel(plan, *refs):
    rows_i, run, c_width, by_partner, tiles_b, groups, steps = plan
    if steps:
        k_hbm, i_hbm, tile_hbm, t_hbm, j_hbm, w_hbm, *refs = refs
        *refs, j_ref, w_sems = refs
    else:
        k_hbm, i_hbm, tile_hbm, t_hbm, *refs = refs
    *refs, k_ref, i_ref, tile_ref, t_ref, small_sems, t_sems = refs
    out_refs = refs[: len(groups)]
    runs = rows_i // run
    rows = CHUNK // runs
    sources, targets = [k_hbm, i_hbm, tile_hbm], [k_ref, i_ref, tile_ref]
    if steps:
        sources.append(j_hbm)
        targets.append(j_ref)
    small_copies = start_all(sources, targets, small_sems)
    me = lax.axis_index("blk") if by_partner else 0
    places = {
        step: (out_ref, spot)
        for out_ref, group in zip(out_refs, groups)
        for spot, step in enumerate(group)
    }
    pairs = [step for step in places if step % 2 == 0]
    columns = [
        pl.ds(pl.multiple_of(((me ^ step) | 1) * TILE - TILE, 2 * TILE), 2 * TILE)
        for step in pairs
    ]
    t_copies = start_all(
        [t_hbm.at[:, span] for span in columns],
        [t_ref.at[n] for n in range(len(pairs))],
        t_sems,
    )
    row = lax.broadcasted_iota(jnp.int32, (rows, CHUNK), 0)
    col = lax.broadcasted_iota(jnp.int32, (rows, CHUNK), 1)
    run_bits = run.bit_length() - 1
    same_c = (row >> run_bits) == (col >> (rows_i.bit_length() - 1))
    same_m = (row & (run - 1)) == (col & (run - 1))
    of_run = jnp.where(same_c & same_m, (col >> run_bits) & (runs - 1), -1)
    own_tile = lax.axis_index("blk") * c_width // TILE
    for copy in small_copies:
        copy.wait()
    w_copies = []
    if steps:
        w_ref, choice_ref = refs[len(groups) :]
        side = lax.axis_index("rep") * tiles_b if by_partner else 0
        flip = len(steps) - tiles_b if by_partner else 0
        label_w = k_ref[0] ^ j_ref[0]
        spot_row = lax.broadcasted_iota(jnp.int32, choice_ref.shape[1:], 0)
        for n in range(len(steps)):
            b_tile = n ^ flip ^ side
            c_tile = place_of(tile_ref, 1, label_w ^ tile_ref[b_tile])
            source = w_hbm.at[
                pl.ds(pl.multiple_of(c_tile * TILE, TILE), TILE),
                pl.ds(pl.multiple_of(b_tile * TILE, TILE), TILE),
            ]
            target = w_ref.at[:, pl.ds(n * TILE, TILE)]
            w_copies.append(pltpu.make_async_copy(source, target, w_sems.at[n]))
            w_copies[-1].start()
            spot = jnp.int32(0)
            for where, step in enumerate(steps):
                spot = jnp.where((c_tile ^ me) == step, jnp.int32(where), spot)
            choice_ref[n] = jnp.where(spot_row == spot, 1.0, 0.0)
    label = k_ref[0] ^ tile_ref[own_tile]
    picks = []
    for step in pairs:
        rows_of_pair = []
        for own in (step, step + 1):
            chosen = place_of(i_ref, run, label ^ tile_ref[me ^ own])
            rows_of_pair.append(jnp.where(of_run == chosen, 1.0, 0.0).astype(jnp.bfloat16))
        picks.append(jnp.concatenate(rows_of_pair, axis=0))
    swapped = (me & 1) == 1
    for n, step in enumerate(pairs):
        t_copies[n].wait()
        for chunk in range(t_ref.shape[1] // CHUNK):
            block = t_ref[n, chunk * CHUNK : (chunk + 1) * CHUNK, :]
            kept = jnp.dot(picks[n], block, preferred_element_type=jnp.float32)
            low, high = kept[:, :TILE], kept[:, TILE:]
            for own, here, other in ((step, low, high), (step + 1, high, low)):
                half = slice((own - step) * rows, (own - step + 1) * rows)
                out_ref, spot = places[own]
                value = jnp.where(swapped, other[half], here[half])
                out_ref[spot, chunk * rows : (chunk + 1) * rows, :] = value.astype(out_ref.dtype)
    for copy in w_copies:
        copy.wait()


def write_coded(out_ref, value):
    rows, width = value.shape
    largest = jnp.max(jnp.max(jnp.abs(value), axis=0, keepdims=True), axis=1, keepdims=True)
    exponent = jnp.ceil(jnp.log2(jnp.maximum(largest, LEAST)))
    scaled = value * (TOP * jnp.exp2(-exponent))
    power = scaled
    for _ in range(POWER.bit_length() - 1):
        power = power * power
    out_ref[:rows, :] = (power * scaled).astype(out_ref.dtype)
    out_ref[rows:, :] = jnp.broadcast_to(exponent, (SPARE, width)).astype(out_ref.dtype)


def read_coded(ref):
    rows = ref.shape[0] - SPARE
    power = ref[:rows, :].astype(jnp.float32)
    exponent = ref[rows:, :].astype(jnp.float32)[:1, :]
    size = jnp.exp2(jnp.log2(jnp.maximum(jnp.abs(power), SMALLEST)) * (1.0 / POWER))
    size = jnp.where(power < 0, -size, size) * (jnp.exp2(exponent) * (1.0 / TOP))
    return jnp.where(power == 0, 0.0, size)


def multiply_kernel(spots, out_count, w_ref, choice_ref, *refs):
    out_refs = refs[-out_count:]
    blocks = [refs[n][spot] for n, spot in spots]
    tiles = choice_ref.shape[0]
    each = tiles // out_count
    for n, out_ref in enumerate(out_refs):
        products = []
        for tile in range(n * each, (n + 1) * each):
            left = jnp.zeros_like(blocks[0])
            for spot, block in enumerate(blocks):
                left = jnp.where(choice_ref[tile, spot : spot + 1, :] > 0.5, block, left)
            products.append(
                lax.dot_general(
                    left,
                    w_ref[:, tile * TILE : (tile + 1) * TILE],
                    (((0,), (0,)), ((), ())),
                    preferred_element_type=jnp.float32,
                )
            )
        value = jnp.concatenate(products, axis=1)
        if out_ref.dtype == jnp.float32:
            out_ref[...] = value
        else:
            write_coded(out_ref, value)


def scale_kernel(
    a_width, i_hbm, j_hbm, tile_hbm, ei_hbm, ej_hbm, ev_ref, after_hbm, denom_ref, run_ref,
    zero_hbm, i_ref, j_ref, tile_ref, ei_ref, ej_ref, column_ref, zero_ref, sems, zero_sems,
):
    copies = start_all(
        (i_hbm, j_hbm, tile_hbm, ei_hbm, ej_hbm), (i_ref, j_ref, tile_ref, ei_ref, ej_ref), sems
    )
    rows_i, b_width = i_ref.shape[0], run_ref.shape[1]
    run = rows_i // tile_ref.shape[0]
    zero_ref[...] = jnp.zeros_like(zero_ref)
    count = zero_ref.shape[0]
    zero_copies = start_all(
        [zero_ref] * (rows_i // count),
        [zero_hbm.at[pl.ds(n * count, count)] for n in range(rows_i // count)],
        zero_sems,
    )
    a_start = lax.axis_index("blk") * a_width
    b_start = lax.axis_index("rep") * b_width
    a_tile = a_start // TILE
    column_ref[...] = jnp.broadcast_to(ev_ref[pl.ds(a_tile, 1), :], (TILE, TILE)).T
    a_energy = column_ref[pl.ds(pl.multiple_of(a_start % TILE, a_width), a_width), :]
    width = min(TILE, b_width)
    for copy in copies:
        copy.wait()
    for part in range(b_width // width):
        b_tile = b_start // TILE + part
        b_tile_row = ev_ref[pl.ds(b_tile, 1), :]
        b_row = b_tile_row[:, :width]
        for n in range(1, TILE // width):
            piece = b_tile_row[:, n * width : (n + 1) * width]
            b_row = jnp.where(b_start % TILE == n * width, piece, b_row)
        chosen = place_of(i_ref, run, j_ref[0] ^ tile_ref[a_tile] ^ tile_ref[b_tile])
        columns = slice(part * width, (part + 1) * width)
        run_ref[:, columns] = jnp.full((run_ref.shape[0], width), chosen.astype(jnp.float32))
        sum_ab = a_energy[:, :width] + b_row
        for m in range(run):
            denom_ref[m * a_width : (m + 1) * a_width, columns] = (
                sum_ab - ei_ref[chosen * run + m] - ej_ref[0]
            )
    for copy in zero_copies:
        copy.wait()


def place_kernel(run, denom_ref, run_ref, zero_hbm, *refs):
    parts_refs, out_hbm, block_ref, sems = refs[:-3], refs[-3], refs[-2], refs[-1]
    a_width, width = block_ref.shape[2:]
    total = parts_refs[-1][...]
    for parts_ref in parts_refs[:-1]:
        coded = parts_ref.dtype != jnp.float32
        total = total + (read_coded(parts_ref) if coded else parts_ref[...])
    scaled = total / denom_ref[...]
    copies = []
    for part in range(block_ref.shape[0]):
        columns = slice(part * width, (part + 1) * width)
        chosen = jnp.max(run_ref[:, columns]).astype(jnp.int32)
        for m in range(run):
            block_ref[part, m] = scaled[m * a_width : (m + 1) * a_width, columns]
        target = out_hbm.at[pl.ds(chosen * run, run), :, pl.ds(part * width, width)]
        copies.append(pltpu.make_async_copy(block_ref.at[part], target, sems.at[part]))
        copies[-1].start()
    for copy in copies:
        copy.wait()


def swap(block, axis, step):
    return lax.ppermute(block, axis, [(n, n ^ step) for n in range(lax.axis_size(axis))])


def shards(t_slab, w_cycle, k_irrep, i_irrep, j_irrep, tile_irrep, i_energy, j_energy, vir_energy):
    blk_count = lax.axis_size("blk")
    rep_count = lax.axis_size("rep")
    k_rows, c_width, rows_i, full_width = t_slab.shape
    rows_j = w_cycle.shape[1]
    assert k_rows == 1 and rows_j == 1
    tiles = tile_irrep.shape[0]
    run = rows_i // tiles
    a_width = full_width // blk_count
    b_width = full_width // rep_count
    deep = c_width * run
    wide = run * a_width
    by_partner = a_width == TILE and b_width % TILE == 0
    steps = list(reversed(range(tiles))) if by_partner else list(range(tiles))
    groups = [[step] for step in steps]
    if by_partner:
        far = [4, 6, 2] if tiles == 8 else range(tiles - 2, 0, -2)
        groups = [[step, step + 1] for step in far] + [[1], [0]]
        steps = [step for group in groups for step in group]

    t_rows = t_slab.reshape(c_width * rows_i, full_width)

    def pack(some_groups, last):
        pairs = sum(len(group) for group in some_groups) // 2
        plan = (rows_i, run, c_width, by_partner, b_width // TILE, some_groups, steps * last)
        arguments = [k_irrep, i_irrep, tile_irrep, t_rows]
        shapes = [
            jax.ShapeDtypeStruct((len(group), deep, TILE), t_slab.dtype) for group in some_groups
        ]
        scratch = [
            small(k_irrep),
            small(i_irrep),
            small(tile_irrep),
            pltpu.VMEM((pairs, t_rows.shape[0], 2 * TILE), t_slab.dtype),
            pltpu.SemaphoreType.DMA((3 + last,)),
            pltpu.SemaphoreType.DMA((pairs,)),
        ]
        if last:
            arguments += [j_irrep, w_cycle.reshape(full_width, full_width)]
            shapes += [
                jax.ShapeDtypeStruct((TILE, full_width), w_cycle.dtype),
                jax.ShapeDtypeStruct((tiles, tiles, TILE), jnp.float32),
            ]
            scratch += [small(j_irrep), pltpu.SemaphoreType.DMA((tiles,))]
        return pl.pallas_call(
            lambda *refs: pack_kernel(plan, *refs),
            in_specs=[hbm()] * len(arguments),
            out_specs=[vmem()] * len(shapes),
            out_shape=shapes,
            scratch_shapes=scratch,
            compiler_params=limit(52 if last else 62),
            name="pack_near" if last else "pack_far",
        )(*arguments)

    packed = list(pack(groups[:3], False)) if by_partner else []
    *near, chosen_w, choice = pack(groups[len(packed) :], True)
    packed += near

    if by_partner:
        *far, beside, own = packed
        left = [swap(pair, "blk", group[0]) for pair, group in zip(far, groups)]
        left += [swap(beside, "blk", 1), own]
        left[0], left[-2], choice = lax.optimization_barrier((left[0], left[-2], choice))
        handed = [swap(pair, "blk", 1) for pair in left[: len(far)]]
        spots = []
        for n in range(len(far)):
            spots += [(n, 0), (len(left) + n, 1)]
        spots += [(len(far), 0), (len(far) + 1, 0)]
        left += handed
        part_shapes = [
            jax.ShapeDtypeStruct((wide + SPARE, b_width), jnp.bfloat16)
        ] * (rep_count - 1) + [jax.ShapeDtypeStruct((wide, b_width), jnp.float32)]
    else:
        stacked = jnp.concatenate(packed).reshape(tiles, c_width, run, TILE // a_width, a_width)
        outgoing = stacked.transpose(0, 3, 1, 2, 4).reshape(blk_count, c_width, wide)
        arrived = lax.all_to_all(outgoing, "blk", split_axis=0, concat_axis=0, tiled=True)
        left = [arrived.reshape(tiles, TILE, wide)]
        spots = [(0, n) for n in range(tiles)]
        part_shapes = [jax.ShapeDtypeStruct((wide, full_width), jnp.float32)]

    partials = pl.pallas_call(
        lambda *refs: multiply_kernel(spots, len(part_shapes), *refs),
        in_specs=[vmem()] * (2 + len(left)),
        out_specs=[vmem()] * len(part_shapes),
        out_shape=part_shapes,
        compiler_params=limit(16),
        name="multiply",
    )(chosen_w, choice, *left)

    out_shape = jax.ShapeDtypeStruct((rows_i, a_width, b_width), jnp.float32)
    denom, run_row, zeros = pl.pallas_call(
        lambda *refs: scale_kernel(a_width, *refs),
        in_specs=[hbm()] * 5 + [vmem(), pl.BlockSpec(memory_space=pl.ANY)],
        out_specs=[vmem(), vmem(), hbm()],
        out_shape=[
            jax.ShapeDtypeStruct((wide, b_width), jnp.float32),
            jax.ShapeDtypeStruct((8, b_width), jnp.float32),
            out_shape,
        ],
        scratch_shapes=[
            small(i_irrep),
            small(j_irrep),
            small(tile_irrep),
            small(i_energy),
            small(j_energy),
            pltpu.VMEM((TILE, TILE), jnp.float32),
            pltpu.VMEM((run, a_width, b_width), jnp.float32),
            pltpu.SemaphoreType.DMA((5,)),
            pltpu.SemaphoreType.DMA((tiles,)),
        ],
        compiler_params=limit(8),
        name="scale",
    )(
        i_irrep, j_irrep, tile_irrep, i_energy, j_energy,
        vir_energy.reshape(full_width // TILE, TILE), partials[-1],
    )

    if by_partner:
        gathered = [
            swap(part, "rep", rep_count - 1 - n) for n, part in enumerate(partials[:-1])
        ] + [partials[-1]]
    else:
        outgoing = partials[0].reshape(wide, rep_count, b_width).transpose(1, 0, 2)
        arrived = lax.all_to_all(outgoing, "rep", split_axis=0, concat_axis=0, tiled=True)
        gathered = [arrived[n] for n in range(rep_count)]

    part_width = min(TILE, b_width)
    result = pl.pallas_call(
        lambda *refs: place_kernel(run, *refs),
        in_specs=[vmem(), vmem(), hbm()] + [vmem()] * rep_count,
        out_specs=hbm(),
        out_shape=out_shape,
        input_output_aliases={2: 0},
        scratch_shapes=[
            pltpu.VMEM((b_width // part_width, run, a_width, part_width), jnp.float32),
            pltpu.SemaphoreType.DMA((b_width // part_width,)),
        ],
        compiler_params=limit(16),
        name="place",
    )(denom, run_row, zeros, *gathered)
    return result.reshape(rows_j, rows_i, a_width, b_width)


def solution(mesh):
    in_specs = (
        P("rep", "blk", None, None),
        P("rep", None, None, None),
        P("rep"),
        P(),
        P(),
        P(),
        P(),
        P(),
        P(),
    )
    out_specs = P(None, None, "blk", "rep")
    return jax.shard_map(shards, mesh=mesh, in_specs=in_specs, out_specs=out_specs, check_vma=False)
```

```python
import jax
import jax.numpy as jnp
from jax import lax
from jax.experimental import pallas as pl
from jax.experimental.pallas import tpu as pltpu
from jax.sharding import PartitionSpec as P

TILE = 128
CHUNK = 256
POWER = 17
TOP = 128.0
LEAST = 2.0**-100
SMALLEST = 2.0**-126
SPARE = 16
PACKED = 16


def vmem():
    return pl.BlockSpec(memory_space=pltpu.VMEM)


def hbm():
    return pl.BlockSpec(memory_space=pltpu.HBM)


def small(array):
    return pltpu.SMEM(array.shape, array.dtype)


def limit(mebibytes):
    return pltpu.CompilerParams(vmem_limit_bytes=mebibytes * 2**20)


def place_of(ref, stride, label):
    found = jnp.int32(0)
    for n in range(ref.shape[0] // stride):
        found = jnp.where(ref[n * stride] == label, jnp.int32(n), found)
    return found


def start_all(sources, targets, sems):
    copies = []
    for n, (source, target) in enumerate(zip(sources, targets)):
        copies.append(pltpu.make_async_copy(source, target, sems.at[n]))
        copies[-1].start()
    return copies


def pack_kernel(plan, *refs):
    rows_i, run, c_width, by_partner, tiles_b, groups, steps = plan
    if steps:
        k_hbm, i_hbm, tile_hbm, t_hbm, j_hbm, w_hbm, *refs = refs
        *refs, j_ref, w_sems = refs
    else:
        k_hbm, i_hbm, tile_hbm, t_hbm, *refs = refs
    *refs, k_ref, i_ref, tile_ref, t_ref, small_sems, t_sems = refs
    out_refs = refs[: len(groups)]
    runs = rows_i // run
    rows = CHUNK // runs
    sources, targets = [k_hbm, i_hbm, tile_hbm], [k_ref, i_ref, tile_ref]
    if steps:
        sources.append(j_hbm)
        targets.append(j_ref)
    small_copies = start_all(sources, targets, small_sems)
    me = lax.axis_index("blk") if by_partner else 0
    places = {
        step: (out_ref, spot)
        for out_ref, group in zip(out_refs, groups)
        for spot, step in enumerate(group)
    }
    pairs = [step for step in places if step % 2 == 0]
    columns = [
        pl.ds(pl.multiple_of(((me ^ step) | 1) * TILE - TILE, 2 * TILE), 2 * TILE)
        for step in pairs
    ]
    t_copies = start_all(
        [t_hbm.at[:, span] for span in columns],
        [t_ref.at[n] for n in range(len(pairs))],
        t_sems,
    )
    row = lax.broadcasted_iota(jnp.int32, (rows, CHUNK), 0)
    col = lax.broadcasted_iota(jnp.int32, (rows, CHUNK), 1)
    run_bits = run.bit_length() - 1
    same_c = (row >> run_bits) == (col >> (rows_i.bit_length() - 1))
    same_m = (row & (run - 1)) == (col & (run - 1))
    of_run = jnp.where(same_c & same_m, (col >> run_bits) & (runs - 1), -1)
    own_tile = lax.axis_index("blk") * c_width // TILE
    for copy in small_copies:
        copy.wait()
    w_copies = []
    if steps:
        w_ref, choice_ref = refs[len(groups) :]
        side = lax.axis_index("rep") * tiles_b if by_partner else 0
        flip = len(steps) - tiles_b if by_partner else 0
        label_w = k_ref[0] ^ j_ref[0]
        for n in range(len(steps)):
            b_tile = n ^ flip ^ side
            c_tile = place_of(tile_ref, 1, label_w ^ tile_ref[b_tile])
            source = w_hbm.at[
                pl.ds(pl.multiple_of(c_tile * TILE, TILE), TILE),
                pl.ds(pl.multiple_of(b_tile * TILE, TILE), TILE),
            ]
            target = w_ref.at[:, pl.ds(n * TILE, TILE)]
            w_copies.append(pltpu.make_async_copy(source, target, w_sems.at[n]))
            w_copies[-1].start()
            for spot, step in enumerate(steps):
                hit = jnp.where((c_tile ^ me) == step, 1.0, 0.0)
                choice_ref[n, spot] = jnp.full((PACKED, TILE), hit).astype(choice_ref.dtype)
    label = k_ref[0] ^ tile_ref[own_tile]
    picks = []
    for step in pairs:
        rows_of_pair = []
        for own in (step, step + 1):
            chosen = place_of(i_ref, run, label ^ tile_ref[me ^ own])
            rows_of_pair.append(jnp.where(of_run == chosen, 1.0, 0.0).astype(jnp.bfloat16))
        picks.append(jnp.concatenate(rows_of_pair, axis=0))
    swapped = (me & 1) == 1
    for n, step in enumerate(pairs):
        t_copies[n].wait()
        for chunk in range(t_ref.shape[1] // CHUNK):
            block = t_ref[n, chunk * CHUNK : (chunk + 1) * CHUNK, :]
            kept = jnp.dot(picks[n], block, preferred_element_type=jnp.float32)
            low, high = kept[:, :TILE], kept[:, TILE:]
            for own, here, other in ((step, low, high), (step + 1, high, low)):
                half = slice((own - step) * rows, (own - step + 1) * rows)
                out_ref, spot = places[own]
                value = jnp.where(swapped, other[half], here[half])
                out_ref[spot, chunk * rows : (chunk + 1) * rows, :] = value.astype(out_ref.dtype)
    for copy in w_copies:
        copy.wait()


def write_coded(out_ref, value):
    rows, width = value.shape
    largest = jnp.max(jnp.abs(value), axis=0, keepdims=True)
    exponent = jnp.ceil(jnp.log2(jnp.maximum(largest, LEAST)))
    scaled = value * (TOP * jnp.exp2(-exponent))
    power = scaled
    for _ in range(POWER.bit_length() - 1):
        power = power * power
    out_ref[:rows, :] = (power * scaled).astype(out_ref.dtype)
    out_ref[rows:, :] = jnp.broadcast_to(exponent, (SPARE, width)).astype(out_ref.dtype)


def read_coded(ref):
    rows = ref.shape[0] - SPARE
    power = ref[:rows, :].astype(jnp.float32)
    exponent = ref[rows:, :].astype(jnp.float32)[:1, :]
    size = jnp.exp2(jnp.log2(jnp.maximum(jnp.abs(power), SMALLEST)) * (1.0 / POWER))
    size = jnp.where(power < 0, -size, size) * (jnp.exp2(exponent) * (1.0 / TOP))
    return jnp.where(power == 0, 0.0, size)


def multiply_kernel(spots, out_count, w_ref, choice_ref, *refs):
    out_refs = refs[-out_count:]
    blocks = [refs[n][spot] for n, spot in spots]
    blocks = [block.reshape(TILE // PACKED, PACKED, block.shape[-1]) for block in blocks]
    tiles = choice_ref.shape[0]
    each = tiles // out_count
    for n, out_ref in enumerate(out_refs):
        products = []
        for tile in range(n * each, (n + 1) * each):
            left = jnp.zeros_like(blocks[0])
            for spot, block in enumerate(blocks):
                left = left + block * choice_ref[tile, spot]
            left = left.reshape(TILE, left.shape[-1])
            products.append(
                lax.dot_general(
                    left,
                    w_ref[:, tile * TILE : (tile + 1) * TILE],
                    (((0,), (0,)), ((), ())),
                    preferred_element_type=jnp.float32,
                )
            )
        value = jnp.concatenate(products, axis=1)
        if out_ref.dtype == jnp.float32:
            out_ref[...] = value
        else:
            write_coded(out_ref, value)


def scale_kernel(
    a_width, i_hbm, j_hbm, tile_hbm, ei_hbm, ej_hbm, ev_ref, after_hbm, denom_ref, run_ref,
    zero_hbm, i_ref, j_ref, tile_ref, ei_ref, ej_ref, column_ref, zero_ref, sems, zero_sems,
):
    copies = start_all(
        (i_hbm, j_hbm, tile_hbm, ei_hbm, ej_hbm), (i_ref, j_ref, tile_ref, ei_ref, ej_ref), sems
    )
    rows_i, b_width = i_ref.shape[0], run_ref.shape[1]
    run = rows_i // tile_ref.shape[0]
    zero_ref[...] = jnp.zeros_like(zero_ref)
    count = zero_ref.shape[0]
    zero_copies = start_all(
        [zero_ref] * (rows_i // count),
        [zero_hbm.at[pl.ds(n * count, count)] for n in range(rows_i // count)],
        zero_sems,
    )
    a_start = lax.axis_index("blk") * a_width
    b_start = lax.axis_index("rep") * b_width
    a_tile = a_start // TILE
    column_ref[...] = jnp.broadcast_to(ev_ref[pl.ds(a_tile, 1), :], (TILE, TILE)).T
    a_energy = column_ref[pl.ds(pl.multiple_of(a_start % TILE, a_width), a_width), :]
    width = min(TILE, b_width)
    for copy in copies:
        copy.wait()
    for part in range(b_width // width):
        b_tile = b_start // TILE + part
        b_tile_row = ev_ref[pl.ds(b_tile, 1), :]
        b_row = b_tile_row[:, :width]
        for n in range(1, TILE // width):
            piece = b_tile_row[:, n * width : (n + 1) * width]
            b_row = jnp.where(b_start % TILE == n * width, piece, b_row)
        chosen = place_of(i_ref, run, j_ref[0] ^ tile_ref[a_tile] ^ tile_ref[b_tile])
        columns = slice(part * width, (part + 1) * width)
        run_ref[:, columns] = jnp.full((run_ref.shape[0], width), chosen.astype(jnp.float32))
        sum_ab = a_energy[:, :width] + b_row
        for m in range(run):
            denom_ref[m * a_width : (m + 1) * a_width, columns] = (
                sum_ab - ei_ref[chosen * run + m] - ej_ref[0]
            )
    for copy in zero_copies:
        copy.wait()


def place_kernel(run, denom_ref, run_ref, zero_hbm, *refs):
    parts_refs, out_hbm, block_ref, sems = refs[:-3], refs[-3], refs[-2], refs[-1]
    a_width, width = block_ref.shape[2:]
    total = parts_refs[-1][...]
    for parts_ref in parts_refs[:-1]:
        coded = parts_ref.dtype != jnp.float32
        total = total + (read_coded(parts_ref) if coded else parts_ref[...])
    scaled = total / denom_ref[...]
    copies = []
    for part in range(block_ref.shape[0]):
        columns = slice(part * width, (part + 1) * width)
        chosen = jnp.max(run_ref[:, columns]).astype(jnp.int32)
        for m in range(run):
            block_ref[part, m] = scaled[m * a_width : (m + 1) * a_width, columns]
        target = out_hbm.at[pl.ds(chosen * run, run), :, pl.ds(part * width, width)]
        copies.append(pltpu.make_async_copy(block_ref.at[part], target, sems.at[part]))
        copies[-1].start()
    for copy in copies:
        copy.wait()


def swap(block, axis, step):
    return lax.ppermute(block, axis, [(n, n ^ step) for n in range(lax.axis_size(axis))])


def shards(t_slab, w_cycle, k_irrep, i_irrep, j_irrep, tile_irrep, i_energy, j_energy, vir_energy):
    blk_count = lax.axis_size("blk")
    rep_count = lax.axis_size("rep")
    k_rows, c_width, rows_i, full_width = t_slab.shape
    rows_j = w_cycle.shape[1]
    assert k_rows == 1 and rows_j == 1
    tiles = tile_irrep.shape[0]
    run = rows_i // tiles
    a_width = full_width // blk_count
    b_width = full_width // rep_count
    deep = c_width * run
    wide = run * a_width
    by_partner = a_width == TILE and b_width % TILE == 0
    steps = list(reversed(range(tiles))) if by_partner else list(range(tiles))
    groups = [[step] for step in steps]
    if by_partner:
        far = [4, 6, 2] if tiles == 8 else range(tiles - 2, 0, -2)
        groups = [[step, step + 1] for step in far] + [[1], [0]]
        steps = [step for group in groups for step in group]

    t_rows = t_slab.reshape(c_width * rows_i, full_width)

    def pack(some_groups, last):
        pairs = sum(len(group) for group in some_groups) // 2
        plan = (rows_i, run, c_width, by_partner, b_width // TILE, some_groups, steps * last)
        arguments = [k_irrep, i_irrep, tile_irrep, t_rows]
        shapes = [
            jax.ShapeDtypeStruct((len(group), deep, TILE), t_slab.dtype) for group in some_groups
        ]
        scratch = [
            small(k_irrep),
            small(i_irrep),
            small(tile_irrep),
            pltpu.VMEM((pairs, t_rows.shape[0], 2 * TILE), t_slab.dtype),
            pltpu.SemaphoreType.DMA((3 + last,)),
            pltpu.SemaphoreType.DMA((pairs,)),
        ]
        if last:
            arguments += [j_irrep, w_cycle.reshape(full_width, full_width)]
            shapes += [
                jax.ShapeDtypeStruct((TILE, full_width), w_cycle.dtype),
                jax.ShapeDtypeStruct((tiles, tiles, PACKED, TILE), t_slab.dtype),
            ]
            scratch += [small(j_irrep), pltpu.SemaphoreType.DMA((tiles,))]
        return pl.pallas_call(
            lambda *refs: pack_kernel(plan, *refs),
            in_specs=[hbm()] * len(arguments),
            out_specs=[vmem()] * len(shapes),
            out_shape=shapes,
            scratch_shapes=scratch,
            compiler_params=limit(52 if last else 62),
            name="pack_near" if last else "pack_far",
        )(*arguments)

    packed = list(pack(groups[:3], False)) if by_partner else []
    *near, chosen_w, choice = pack(groups[len(packed) :], True)
    packed += near

    if by_partner:
        *far, beside, own = packed
        left = [swap(pair, "blk", group[0]) for pair, group in zip(far, groups)]
        left += [swap(beside, "blk", 1), own]
        left[0], left[-2], choice = lax.optimization_barrier((left[0], left[-2], choice))
        handed = [swap(pair, "blk", 1) for pair in left[: len(far)]]
        spots = []
        for n in range(len(far)):
            spots += [(n, 0), (len(left) + n, 1)]
        spots += [(len(far), 0), (len(far) + 1, 0)]
        left += handed
        part_shapes = [
            jax.ShapeDtypeStruct((wide + SPARE, b_width), jnp.bfloat16)
        ] * (rep_count - 1) + [jax.ShapeDtypeStruct((wide, b_width), jnp.float32)]
    else:
        stacked = jnp.concatenate(packed).reshape(tiles, c_width, run, TILE // a_width, a_width)
        outgoing = stacked.transpose(0, 3, 1, 2, 4).reshape(blk_count, c_width, wide)
        arrived = lax.all_to_all(outgoing, "blk", split_axis=0, concat_axis=0, tiled=True)
        left = [arrived.reshape(tiles, TILE, wide)]
        spots = [(0, n) for n in range(tiles)]
        part_shapes = [jax.ShapeDtypeStruct((wide, full_width), jnp.float32)]

    partials = pl.pallas_call(
        lambda *refs: multiply_kernel(spots, len(part_shapes), *refs),
        in_specs=[vmem()] * (2 + len(left)),
        out_specs=[vmem()] * len(part_shapes),
        out_shape=part_shapes,
        compiler_params=limit(16),
        name="multiply",
    )(chosen_w, choice, *left)

    out_shape = jax.ShapeDtypeStruct((rows_i, a_width, b_width), jnp.float32)
    denom, run_row, zeros = pl.pallas_call(
        lambda *refs: scale_kernel(a_width, *refs),
        in_specs=[hbm()] * 5 + [vmem(), pl.BlockSpec(memory_space=pl.ANY)],
        out_specs=[vmem(), vmem(), hbm()],
        out_shape=[
            jax.ShapeDtypeStruct((wide, b_width), jnp.float32),
            jax.ShapeDtypeStruct((8, b_width), jnp.float32),
            out_shape,
        ],
        scratch_shapes=[
            small(i_irrep),
            small(j_irrep),
            small(tile_irrep),
            small(i_energy),
            small(j_energy),
            pltpu.VMEM((TILE, TILE), jnp.float32),
            pltpu.VMEM((run, a_width, b_width), jnp.float32),
            pltpu.SemaphoreType.DMA((5,)),
            pltpu.SemaphoreType.DMA((tiles,)),
        ],
        compiler_params=limit(8),
        name="scale",
    )(
        i_irrep, j_irrep, tile_irrep, i_energy, j_energy,
        vir_energy.reshape(full_width // TILE, TILE), partials[-1],
    )

    if by_partner:
        gathered = [
            swap(part, "rep", rep_count - 1 - n) for n, part in enumerate(partials[:-1])
        ] + [partials[-1]]
    else:
        outgoing = partials[0].reshape(wide, rep_count, b_width).transpose(1, 0, 2)
        arrived = lax.all_to_all(outgoing, "rep", split_axis=0, concat_axis=0, tiled=True)
        gathered = [arrived[n] for n in range(rep_count)]

    part_width = min(TILE, b_width)
    result = pl.pallas_call(
        lambda *refs: place_kernel(run, *refs),
        in_specs=[vmem(), vmem(), hbm()] + [vmem()] * rep_count,
        out_specs=hbm(),
        out_shape=out_shape,
        input_output_aliases={2: 0},
        scratch_shapes=[
            pltpu.VMEM((b_width // part_width, run, a_width, part_width), jnp.float32),
            pltpu.SemaphoreType.DMA((b_width // part_width,)),
        ],
        compiler_params=limit(16),
        name="place",
    )(denom, run_row, zeros, *gathered)
    return result.reshape(rows_j, rows_i, a_width, b_width)


def solution(mesh):
    in_specs = (
        P("rep", "blk", None, None),
        P("rep", None, None, None),
        P("rep"),
        P(),
        P(),
        P(),
        P(),
        P(),
        P(),
    )
    out_specs = P(None, None, "blk", "rep")
    return jax.shard_map(shards, mesh=mesh, in_specs=in_specs, out_specs=out_specs, check_vma=False)
```

```python
import jax
import jax.numpy as jnp
from jax import lax
from jax.experimental import pallas as pl
from jax.experimental.pallas import tpu as pltpu
from jax.sharding import PartitionSpec as P

TILE = 128
CHUNK = 256
POWER = 17
TOP = 128.0
LEAST = 2.0**-100
SMALLEST = 2.0**-126
SPARE = 16


def vmem():
    return pl.BlockSpec(memory_space=pltpu.VMEM)


def hbm():
    return pl.BlockSpec(memory_space=pltpu.HBM)


def small(array):
    return pltpu.SMEM(array.shape, array.dtype)


def limit(mebibytes):
    return pltpu.CompilerParams(vmem_limit_bytes=mebibytes * 2**20)


def place_of(ref, stride, label):
    found = jnp.int32(0)
    for n in range(ref.shape[0] // stride):
        found = jnp.where(ref[n * stride] == label, jnp.int32(n), found)
    return found


def tabulate(table_ref, ref, stride):
    for n in range(table_ref.shape[0]):
        table_ref[ref[n * stride]] = jnp.int32(n)


def start_all(sources, targets, sems):
    copies = []
    for n, (source, target) in enumerate(zip(sources, targets)):
        copies.append(pltpu.make_async_copy(source, target, sems.at[n]))
        copies[-1].start()
    return copies


def pack_kernel(plan, *refs):
    rows_i, run, c_width, by_partner, tiles_b, groups, steps = plan
    if steps:
        k_ref, j_ref, i_hbm, tile_hbm, t_hbm, w_hbm, *refs = refs
        *refs, tile_of_ref, w_sems = refs
    else:
        k_ref, i_hbm, tile_hbm, t_hbm, *refs = refs
    *refs, i_ref, tile_ref, run_of_ref, t_ref, small_sems, t_sems = refs
    out_refs = refs[: len(groups)]
    runs = rows_i // run
    rows = CHUNK // runs
    small_copies = start_all((i_hbm, tile_hbm), (i_ref, tile_ref), small_sems)
    me = lax.axis_index("blk") if by_partner else 0
    places = {
        step: (out_ref, spot)
        for out_ref, group in zip(out_refs, groups)
        for spot, step in enumerate(group)
    }
    pairs = [step for step in places if step % 2 == 0]
    columns = [
        pl.ds(pl.multiple_of(((me ^ step) | 1) * TILE - TILE, 2 * TILE), 2 * TILE)
        for step in pairs
    ]
    t_copies = start_all(
        [t_hbm.at[:, span] for span in columns],
        [t_ref.at[n] for n in range(len(pairs))],
        t_sems,
    )
    row = lax.broadcasted_iota(jnp.int32, (rows, CHUNK), 0)
    col = lax.broadcasted_iota(jnp.int32, (rows, CHUNK), 1)
    run_bits = run.bit_length() - 1
    same_c = (row >> run_bits) == (col >> (rows_i.bit_length() - 1))
    same_m = (row & (run - 1)) == (col & (run - 1))
    of_run = jnp.where(same_c & same_m, (col >> run_bits) & (runs - 1), -1)
    own_tile = lax.axis_index("blk") * c_width // TILE
    for copy in small_copies:
        copy.wait()
    tabulate(run_of_ref, i_ref, run)
    w_copies = []
    if steps:
        tabulate(tile_of_ref, tile_ref, 1)
        w_ref, choice_ref = refs[len(groups) :]
        side = lax.axis_index("rep") * tiles_b if by_partner else 0
        flip = len(steps) - tiles_b if by_partner else 0
        label_w = k_ref[0] ^ j_ref[0]
        spot_row = lax.broadcasted_iota(jnp.int32, choice_ref.shape[1:], 0)
        for n in range(len(steps)):
            b_tile = n ^ flip ^ side
            c_tile = tile_of_ref[label_w ^ tile_ref[b_tile]]
            source = w_hbm.at[
                pl.ds(pl.multiple_of(c_tile * TILE, TILE), TILE),
                pl.ds(pl.multiple_of(b_tile * TILE, TILE), TILE),
            ]
            target = w_ref.at[:, pl.ds(n * TILE, TILE)]
            w_copies.append(pltpu.make_async_copy(source, target, w_sems.at[n]))
            w_copies[-1].start()
            spot = jnp.int32(0)
            for where, step in enumerate(steps):
                spot = jnp.where((c_tile ^ me) == step, jnp.int32(where), spot)
            choice_ref[n] = jnp.where(spot_row == spot, 1.0, 0.0)
    label = k_ref[0] ^ tile_ref[own_tile]
    picks = []
    for step in pairs:
        rows_of_pair = []
        for own in (step, step + 1):
            chosen = run_of_ref[label ^ tile_ref[me ^ own]]
            rows_of_pair.append(jnp.where(of_run == chosen, 1.0, 0.0).astype(jnp.bfloat16))
        picks.append(jnp.concatenate(rows_of_pair, axis=0))
    swapped = (me & 1) == 1
    for n, step in enumerate(pairs):
        t_copies[n].wait()
        for chunk in range(t_ref.shape[1] // CHUNK):
            block = t_ref[n, chunk * CHUNK : (chunk + 1) * CHUNK, :]
            kept = jnp.dot(picks[n], block, preferred_element_type=jnp.float32)
            low, high = kept[:, :TILE], kept[:, TILE:]
            for own, here, other in ((step, low, high), (step + 1, high, low)):
                half = slice((own - step) * rows, (own - step + 1) * rows)
                out_ref, spot = places[own]
                value = jnp.where(swapped, other[half], here[half])
                out_ref[spot, chunk * rows : (chunk + 1) * rows, :] = value.astype(out_ref.dtype)
    for copy in w_copies:
        copy.wait()


def write_coded(out_ref, value):
    rows, width = value.shape
    largest = jnp.max(jnp.max(jnp.abs(value), axis=0, keepdims=True), axis=1, keepdims=True)
    exponent = jnp.ceil(jnp.log2(jnp.maximum(largest, LEAST)))
    scaled = value * (TOP * jnp.exp2(-exponent))
    power = scaled
    for _ in range(POWER.bit_length() - 1):
        power = power * power
    out_ref[:rows, :] = (power * scaled).astype(out_ref.dtype)
    out_ref[rows:, :] = jnp.broadcast_to(exponent, (SPARE, width)).astype(out_ref.dtype)


def read_coded(ref):
    rows = ref.shape[0] - SPARE
    power = ref[:rows, :].astype(jnp.float32)
    exponent = ref[rows:, :].astype(jnp.float32)[:1, :]
    size = jnp.exp2(jnp.log2(jnp.maximum(jnp.abs(power), SMALLEST)) * (1.0 / POWER))
    size = jnp.where(power < 0, -size, size) * (jnp.exp2(exponent) * (1.0 / TOP))
    return jnp.where(power == 0, 0.0, size)


def multiply_kernel(spots, out_count, w_ref, choice_ref, *refs):
    out_refs = refs[-out_count:]
    blocks = [refs[n][spot] for n, spot in spots]
    tiles = choice_ref.shape[0]
    each = tiles // out_count
    for n, out_ref in enumerate(out_refs):
        products = []
        for tile in range(n * each, (n + 1) * each):
            left = jnp.zeros_like(blocks[0])
            for spot, block in enumerate(blocks):
                chosen = choice_ref[tile, spot : spot + 1, :]
                if block.shape[1] != TILE:
                    chosen = jnp.broadcast_to(chosen[:, :1], (1, block.shape[1]))
                left = jnp.where(chosen > 0.5, block, left)
            products.append(
                lax.dot_general(
                    left,
                    w_ref[:, tile * TILE : (tile + 1) * TILE],
                    (((0,), (0,)), ((), ())),
                    preferred_element_type=jnp.float32,
                )
            )
        value = jnp.concatenate(products, axis=1)
        if out_ref.dtype == jnp.float32:
            out_ref[...] = value
        else:
            write_coded(out_ref, value)


def scale_kernel(
    a_width, i_hbm, j_hbm, tile_hbm, ei_hbm, ej_hbm, ev_ref, after_hbm, denom_ref, run_ref,
    zero_hbm, i_ref, j_ref, tile_ref, ei_ref, ej_ref, column_ref, zero_ref, sems, zero_sems,
):
    copies = start_all(
        (i_hbm, j_hbm, tile_hbm, ei_hbm, ej_hbm), (i_ref, j_ref, tile_ref, ei_ref, ej_ref), sems
    )
    rows_i, b_width = i_ref.shape[0], run_ref.shape[1]
    run = rows_i // tile_ref.shape[0]
    zero_ref[...] = jnp.zeros_like(zero_ref)
    count = zero_ref.shape[0]
    zero_copies = start_all(
        [zero_ref] * (rows_i // count),
        [zero_hbm.at[pl.ds(n * count, count)] for n in range(rows_i // count)],
        zero_sems,
    )
    a_start = lax.axis_index("blk") * a_width
    b_start = lax.axis_index("rep") * b_width
    a_tile = a_start // TILE
    column_ref[...] = jnp.broadcast_to(ev_ref[pl.ds(a_tile, 1), :], (TILE, TILE)).T
    a_energy = column_ref[pl.ds(pl.multiple_of(a_start % TILE, a_width), a_width), :]
    width = min(TILE, b_width)
    for copy in copies:
        copy.wait()
    for part in range(b_width // width):
        b_tile = b_start // TILE + part
        b_tile_row = ev_ref[pl.ds(b_tile, 1), :]
        b_row = b_tile_row[:, :width]
        for n in range(1, TILE // width):
            piece = b_tile_row[:, n * width : (n + 1) * width]
            b_row = jnp.where(b_start % TILE == n * width, piece, b_row)
        chosen = place_of(i_ref, run, j_ref[0] ^ tile_ref[a_tile] ^ tile_ref[b_tile])
        columns = slice(part * width, (part + 1) * width)
        run_ref[:, columns] = jnp.full((run_ref.shape[0], width), chosen.astype(jnp.float32))
        sum_ab = a_energy[:, :width] + b_row
        for m in range(run):
            denom_ref[m * a_width : (m + 1) * a_width, columns] = (
                sum_ab - ei_ref[chosen * run + m] - ej_ref[0]
            )
    for copy in zero_copies:
        copy.wait()


def place_kernel(run, denom_ref, run_ref, zero_hbm, *refs):
    parts_refs, out_hbm, block_ref, sems = refs[:-3], refs[-3], refs[-2], refs[-1]
    a_width, width = block_ref.shape[2:]
    total = parts_refs[-1][...]
    for parts_ref in parts_refs[:-1]:
        coded = parts_ref.dtype != jnp.float32
        total = total + (read_coded(parts_ref) if coded else parts_ref[...])
    scaled = total / denom_ref[...]
    copies = []
    for part in range(block_ref.shape[0]):
        columns = slice(part * width, (part + 1) * width)
        chosen = jnp.max(run_ref[:, columns]).astype(jnp.int32)
        for m in range(run):
            block_ref[part, m] = scaled[m * a_width : (m + 1) * a_width, columns]
        target = out_hbm.at[pl.ds(chosen * run, run), :, pl.ds(part * width, width)]
        copies.append(pltpu.make_async_copy(block_ref.at[part], target, sems.at[part]))
        copies[-1].start()
    for copy in copies:
        copy.wait()


def swap(block, axis, step):
    return lax.ppermute(block, axis, [(n, n ^ step) for n in range(lax.axis_size(axis))])


def shards(t_slab, w_cycle, k_irrep, i_irrep, j_irrep, tile_irrep, i_energy, j_energy, vir_energy):
    blk_count = lax.axis_size("blk")
    rep_count = lax.axis_size("rep")
    k_rows, c_width, rows_i, full_width = t_slab.shape
    rows_j = w_cycle.shape[1]
    assert k_rows == 1 and rows_j == 1
    tiles = tile_irrep.shape[0]
    run = rows_i // tiles
    a_width = full_width // blk_count
    b_width = full_width // rep_count
    deep = c_width * run
    wide = run * a_width
    by_partner = a_width == TILE and b_width % TILE == 0 and run == 1
    steps = list(reversed(range(tiles))) if by_partner else list(range(tiles))
    groups = [[step] for step in steps]
    if by_partner:
        far = [4, 6, 2] if tiles == 8 else range(tiles - 2, 0, -2)
        groups = [[step, step + 1] for step in far] + [[1], [0]]
        steps = [step for group in groups for step in group]

    t_rows = t_slab.reshape(c_width * rows_i, full_width)

    def pack(some_groups, last):
        pairs = sum(len(group) for group in some_groups) // 2
        plan = (rows_i, run, c_width, by_partner, b_width // TILE, some_groups, steps * last)
        arguments = [i_irrep, tile_irrep, t_rows]
        scalars = [k_irrep]
        shapes = [
            jax.ShapeDtypeStruct((len(group), deep, TILE), t_slab.dtype) for group in some_groups
        ]
        scratch = [
            small(i_irrep),
            small(tile_irrep),
            small(tile_irrep),
            pltpu.VMEM((pairs, t_rows.shape[0], 2 * TILE), t_slab.dtype),
            pltpu.SemaphoreType.DMA((2,)),
            pltpu.SemaphoreType.DMA((pairs,)),
        ]
        if last:
            arguments.append(w_cycle.reshape(full_width, full_width))
            scalars.append(j_irrep)
            shapes += [
                jax.ShapeDtypeStruct((TILE, full_width), w_cycle.dtype),
                jax.ShapeDtypeStruct((tiles, tiles, TILE), jnp.float32),
            ]
            scratch += [small(tile_irrep), pltpu.SemaphoreType.DMA((tiles,))]
        return pl.pallas_call(
            lambda *refs: pack_kernel(plan, *refs),
            in_specs=[pl.BlockSpec(memory_space=pltpu.SMEM)] * len(scalars)
            + [hbm()] * len(arguments),
            out_specs=[vmem()] * len(shapes),
            out_shape=shapes,
            scratch_shapes=scratch,
            compiler_params=limit(52 if last else 62),
            name="pack_near" if last else "pack_far",
        )(*scalars, *arguments)

    packed = list(pack(groups[:3], False)) if by_partner else []
    *near, chosen_w, choice = pack(groups[len(packed) :], True)
    packed += near

    if by_partner:
        *far, beside, own = packed
        left = [swap(pair, "blk", group[0]) for pair, group in zip(far, groups)]
        left += [swap(beside, "blk", 1), own]
        left[0], left[-2], choice = lax.optimization_barrier((left[0], left[-2], choice))
        handed = [swap(pair, "blk", 1) for pair in left[: len(far)]]
        spots = []
        for n in range(len(far)):
            spots += [(n, 0), (len(left) + n, 1)]
        spots += [(len(far), 0), (len(far) + 1, 0)]
        left += handed
        part_shapes = [
            jax.ShapeDtypeStruct((wide + SPARE, b_width), jnp.bfloat16)
        ] * (rep_count - 1) + [jax.ShapeDtypeStruct((wide, b_width), jnp.float32)]
    else:
        stacked = jnp.concatenate(packed).reshape(tiles, c_width, run, TILE // a_width, a_width)
        outgoing = stacked.transpose(0, 3, 1, 2, 4).reshape(blk_count, c_width, wide)
        arrived = lax.all_to_all(outgoing, "blk", split_axis=0, concat_axis=0, tiled=True)
        left = [arrived.reshape(tiles, TILE, wide)]
        spots = [(0, n) for n in range(tiles)]
        part_shapes = [jax.ShapeDtypeStruct((wide, full_width), jnp.float32)]

    partials = pl.pallas_call(
        lambda *refs: multiply_kernel(spots, len(part_shapes), *refs),
        in_specs=[vmem()] * (2 + len(left)),
        out_specs=[vmem()] * len(part_shapes),
        out_shape=part_shapes,
        compiler_params=limit(16),
        name="multiply",
    )(chosen_w, choice, *left)

    out_shape = jax.ShapeDtypeStruct((rows_i, a_width, b_width), jnp.float32)
    denom, run_row, zeros = pl.pallas_call(
        lambda *refs: scale_kernel(a_width, *refs),
        in_specs=[hbm()] * 5 + [vmem(), pl.BlockSpec(memory_space=pl.ANY)],
        out_specs=[vmem(), vmem(), hbm()],
        out_shape=[
            jax.ShapeDtypeStruct((wide, b_width), jnp.float32),
            jax.ShapeDtypeStruct((8, b_width), jnp.float32),
            out_shape,
        ],
        scratch_shapes=[
            small(i_irrep),
            small(j_irrep),
            small(tile_irrep),
            small(i_energy),
            small(j_energy),
            pltpu.VMEM((TILE, TILE), jnp.float32),
            pltpu.VMEM((run, a_width, b_width), jnp.float32),
            pltpu.SemaphoreType.DMA((5,)),
            pltpu.SemaphoreType.DMA((tiles,)),
        ],
        compiler_params=limit(8),
        name="scale",
    )(
        i_irrep, j_irrep, tile_irrep, i_energy, j_energy,
        vir_energy.reshape(full_width // TILE, TILE), partials[-1],
    )

    if by_partner:
        gathered = [
            swap(part, "rep", rep_count - 1 - n) for n, part in enumerate(partials[:-1])
        ] + [partials[-1]]
    else:
        outgoing = partials[0].reshape(wide, rep_count, b_width).transpose(1, 0, 2)
        arrived = lax.all_to_all(outgoing, "rep", split_axis=0, concat_axis=0, tiled=True)
        gathered = [arrived[n] for n in range(rep_count)]

    part_width = min(TILE, b_width)
    result = pl.pallas_call(
        lambda *refs: place_kernel(run, *refs),
        in_specs=[vmem(), vmem(), hbm()] + [vmem()] * rep_count,
        out_specs=hbm(),
        out_shape=out_shape,
        input_output_aliases={2: 0},
        scratch_shapes=[
            pltpu.VMEM((b_width // part_width, run, a_width, part_width), jnp.float32),
            pltpu.SemaphoreType.DMA((b_width // part_width,)),
        ],
        compiler_params=limit(16),
        name="place",
    )(denom, run_row, zeros, *gathered)
    return result.reshape(rows_j, rows_i, a_width, b_width)


def solution(mesh):
    in_specs = (
        P("rep", "blk", None, None),
        P("rep", None, None, None),
        P("rep"),
        P(),
        P(),
        P(),
        P(),
        P(),
        P(),
    )
    out_specs = P(None, None, "blk", "rep")
    return jax.shard_map(shards, mesh=mesh, in_specs=in_specs, out_specs=out_specs, check_vma=False)
```

```python
import jax
import jax.numpy as jnp
from jax import lax
from jax.experimental import pallas as pl
from jax.experimental.pallas import tpu as pltpu
from jax.sharding import PartitionSpec as P

TILE = 128
CHUNK = 256
POWER = 17
TOP = 128.0
LEAST = 2.0**-100
SMALLEST = 2.0**-126
SPARE = 16


def vmem():
    return pl.BlockSpec(memory_space=pltpu.VMEM)


def hbm():
    return pl.BlockSpec(memory_space=pltpu.HBM)


def small(array):
    return pltpu.SMEM(array.shape, array.dtype)


def limit(mebibytes):
    return pltpu.CompilerParams(vmem_limit_bytes=mebibytes * 2**20)


def place_of(ref, stride, label):
    found = jnp.int32(0)
    for n in range(ref.shape[0] // stride):
        found = jnp.where(ref[n * stride] == label, jnp.int32(n), found)
    return found


def start_all(sources, targets, sems):
    copies = []
    for n, (source, target) in enumerate(zip(sources, targets)):
        copies.append(pltpu.make_async_copy(source, target, sems.at[n]))
        copies[-1].start()
    return copies


def pack_kernel(plan, *refs):
    rows_i, run, c_width, by_partner, tiles_b, groups, steps = plan
    if steps:
        k_hbm, i_hbm, tile_hbm, t_hbm, j_hbm, w_hbm, *refs = refs
        *refs, j_ref, w_sems = refs
    else:
        k_hbm, i_hbm, tile_hbm, t_hbm, *refs = refs
    *refs, k_ref, i_ref, tile_ref, t_ref, small_sems, t_sems = refs
    out_refs = refs[: len(groups)]
    runs = rows_i // run
    rows = CHUNK // runs
    sources, targets = [k_hbm, i_hbm, tile_hbm], [k_ref, i_ref, tile_ref]
    if steps:
        sources.append(j_hbm)
        targets.append(j_ref)
    small_copies = start_all(sources, targets, small_sems)
    me = lax.axis_index("blk") if by_partner else 0
    places = {
        step: (out_ref, spot)
        for out_ref, group in zip(out_refs, groups)
        for spot, step in enumerate(group)
    }
    pairs = [step for step in places if step % 2 == 0]
    columns = [
        pl.ds(pl.multiple_of(((me ^ step) | 1) * TILE - TILE, 2 * TILE), 2 * TILE)
        for step in pairs
    ]
    t_copies = start_all(
        [t_hbm.at[:, span] for span in columns],
        [t_ref.at[n] for n in range(len(pairs))],
        t_sems,
    )
    row = lax.broadcasted_iota(jnp.int32, (rows, CHUNK), 0)
    col = lax.broadcasted_iota(jnp.int32, (rows, CHUNK), 1)
    run_bits = run.bit_length() - 1
    same_c = (row >> run_bits) == (col >> (rows_i.bit_length() - 1))
    same_m = (row & (run - 1)) == (col & (run - 1))
    of_run = jnp.where(same_c & same_m, (col >> run_bits) & (runs - 1), -1)
    own_tile = lax.axis_index("blk") * c_width // TILE
    for copy in small_copies:
        copy.wait()
    w_copies = []
    if steps:
        w_ref, choice_ref = refs[len(groups) :]
        side = lax.axis_index("rep") * tiles_b if by_partner else 0
        flip = len(steps) - tiles_b if by_partner else 0
        label_w = k_ref[0] ^ j_ref[0]
        spot_row = lax.broadcasted_iota(jnp.int32, choice_ref.shape[1:], 0)
        for n in range(len(steps)):
            b_tile = n ^ flip ^ side
            c_tile = place_of(tile_ref, 1, label_w ^ tile_ref[b_tile])
            source = w_hbm.at[
                pl.ds(pl.multiple_of(c_tile * TILE, TILE), TILE),
                pl.ds(pl.multiple_of(b_tile * TILE, TILE), TILE),
            ]
            target = w_ref.at[:, pl.ds(n * TILE, TILE)]
            w_copies.append(pltpu.make_async_copy(source, target, w_sems.at[n]))
            w_copies[-1].start()
            spot = jnp.int32(0)
            for where, step in enumerate(steps):
                spot = jnp.where((c_tile ^ me) == step, jnp.int32(where), spot)
            choice_ref[n] = jnp.where(spot_row == spot, 1.0, 0.0)
    label = k_ref[0] ^ tile_ref[own_tile]
    picks = []
    for step in pairs:
        rows_of_pair = []
        for own in (step, step + 1):
            chosen = place_of(i_ref, run, label ^ tile_ref[me ^ own])
            rows_of_pair.append(jnp.where(of_run == chosen, 1.0, 0.0).astype(jnp.bfloat16))
        picks.append(jnp.concatenate(rows_of_pair, axis=0))
    swapped = (me & 1) == 1
    for n, step in enumerate(pairs):
        t_copies[n].wait()
        for chunk in range(t_ref.shape[1] // CHUNK):
            block = t_ref[n, chunk * CHUNK : (chunk + 1) * CHUNK, :]
            kept = jnp.dot(picks[n], block, preferred_element_type=jnp.float32)
            low, high = kept[:, :TILE], kept[:, TILE:]
            for own, here, other in ((step, low, high), (step + 1, high, low)):
                half = slice((own - step) * rows, (own - step + 1) * rows)
                out_ref, spot = places[own]
                value = jnp.where(swapped, other[half], here[half])
                out_ref[spot, chunk * rows : (chunk + 1) * rows, :] = value.astype(out_ref.dtype)
    for copy in w_copies:
        copy.wait()


def write_coded(out_ref, value):
    rows, width = value.shape
    largest = jnp.max(jnp.max(jnp.abs(value), axis=0, keepdims=True), axis=1, keepdims=True)
    exponent = jnp.ceil(jnp.log2(jnp.maximum(largest, LEAST)))
    scaled = value * (TOP * jnp.exp2(-exponent))
    power = scaled
    for _ in range(POWER.bit_length() - 1):
        power = power * power
    out_ref[:rows, :] = (power * scaled).astype(out_ref.dtype)
    out_ref[rows:, :] = jnp.broadcast_to(exponent, (SPARE, width)).astype(out_ref.dtype)


def read_coded(ref):
    rows = ref.shape[0] - SPARE
    power = ref[:rows, :].astype(jnp.float32)
    exponent = ref[rows:, :].astype(jnp.float32)[:1, :]
    size = jnp.exp2(jnp.log2(jnp.maximum(jnp.abs(power), SMALLEST)) * (1.0 / POWER))
    size = jnp.where(power < 0, -size, size) * (jnp.exp2(exponent) * (1.0 / TOP))
    return jnp.where(power == 0, 0.0, size)


def second_kernel(pair_ref, out_ref):
    out_ref[...] = pair_ref[1:]


def multiply_kernel(spots, out_count, w_ref, choice_ref, *refs):
    out_refs = refs[-out_count:]
    blocks = [refs[n][spot] for n, spot in spots]
    tiles = choice_ref.shape[0]
    each = tiles // out_count
    for n, out_ref in enumerate(out_refs):
        products = []
        for tile in range(n * each, (n + 1) * each):
            left = jnp.zeros_like(blocks[0])
            for spot, block in enumerate(blocks):
                left = jnp.where(choice_ref[tile, spot : spot + 1, :] > 0.5, block, left)
            products.append(
                lax.dot_general(
                    left,
                    w_ref[:, tile * TILE : (tile + 1) * TILE],
                    (((0,), (0,)), ((), ())),
                    preferred_element_type=jnp.float32,
                )
            )
        value = jnp.concatenate(products, axis=1)
        if out_ref.dtype == jnp.float32:
            out_ref[...] = value
        else:
            write_coded(out_ref, value)


def scale_kernel(
    a_width, i_hbm, j_hbm, tile_hbm, ei_hbm, ej_hbm, ev_ref, after_hbm, denom_ref, run_ref,
    zero_hbm, i_ref, j_ref, tile_ref, ei_ref, ej_ref, column_ref, zero_ref, sems, zero_sems,
):
    copies = start_all(
        (i_hbm, j_hbm, tile_hbm, ei_hbm, ej_hbm), (i_ref, j_ref, tile_ref, ei_ref, ej_ref), sems
    )
    rows_i, b_width = i_ref.shape[0], run_ref.shape[1]
    run = rows_i // tile_ref.shape[0]
    zero_ref[...] = jnp.zeros_like(zero_ref)
    count = zero_ref.shape[0]
    zero_copies = start_all(
        [zero_ref] * (rows_i // count),
        [zero_hbm.at[pl.ds(n * count, count)] for n in range(rows_i // count)],
        zero_sems,
    )
    a_start = lax.axis_index("blk") * a_width
    b_start = lax.axis_index("rep") * b_width
    a_tile = a_start // TILE
    column_ref[...] = jnp.broadcast_to(ev_ref[pl.ds(a_tile, 1), :], (TILE, TILE)).T
    a_energy = column_ref[pl.ds(pl.multiple_of(a_start % TILE, a_width), a_width), :]
    width = min(TILE, b_width)
    for copy in copies:
        copy.wait()
    for part in range(b_width // width):
        b_tile = b_start // TILE + part
        b_tile_row = ev_ref[pl.ds(b_tile, 1), :]
        b_row = b_tile_row[:, :width]
        for n in range(1, TILE // width):
            piece = b_tile_row[:, n * width : (n + 1) * width]
            b_row = jnp.where(b_start % TILE == n * width, piece, b_row)
        chosen = place_of(i_ref, run, j_ref[0] ^ tile_ref[a_tile] ^ tile_ref[b_tile])
        columns = slice(part * width, (part + 1) * width)
        run_ref[:, columns] = jnp.full((run_ref.shape[0], width), chosen.astype(jnp.float32))
        sum_ab = a_energy[:, :width] + b_row
        for m in range(run):
            denom_ref[m * a_width : (m + 1) * a_width, columns] = (
                sum_ab - ei_ref[chosen * run + m] - ej_ref[0]
            )
    for copy in zero_copies:
        copy.wait()


def add_kernel(part_ref, so_far_ref, out_ref):
    out_ref[...] = so_far_ref[...] + read_coded(part_ref)


def place_kernel(run, denom_ref, run_ref, zero_hbm, *refs):
    parts_refs, out_hbm, block_ref, sems = refs[:-3], refs[-3], refs[-2], refs[-1]
    a_width, width = block_ref.shape[2:]
    total = parts_refs[-1][...]
    for parts_ref in parts_refs[:-1]:
        coded = parts_ref.dtype != jnp.float32
        total = total + (read_coded(parts_ref) if coded else parts_ref[...])
    scaled = total / denom_ref[...]
    copies = []
    for part in range(block_ref.shape[0]):
        columns = slice(part * width, (part + 1) * width)
        chosen = jnp.max(run_ref[:, columns]).astype(jnp.int32)
        for m in range(run):
            block_ref[part, m] = scaled[m * a_width : (m + 1) * a_width, columns]
        target = out_hbm.at[pl.ds(chosen * run, run), :, pl.ds(part * width, width)]
        copies.append(pltpu.make_async_copy(block_ref.at[part], target, sems.at[part]))
        copies[-1].start()
    for copy in copies:
        copy.wait()


def swap(block, axis, step):
    return lax.ppermute(block, axis, [(n, n ^ step) for n in range(lax.axis_size(axis))])


def shards(t_slab, w_cycle, k_irrep, i_irrep, j_irrep, tile_irrep, i_energy, j_energy, vir_energy):
    blk_count = lax.axis_size("blk")
    rep_count = lax.axis_size("rep")
    k_rows, c_width, rows_i, full_width = t_slab.shape
    rows_j = w_cycle.shape[1]
    assert k_rows == 1 and rows_j == 1
    tiles = tile_irrep.shape[0]
    run = rows_i // tiles
    a_width = full_width // blk_count
    b_width = full_width // rep_count
    deep = c_width * run
    wide = run * a_width
    by_partner = a_width == TILE and b_width % TILE == 0 and run == 1
    steps = list(reversed(range(tiles))) if by_partner else list(range(tiles))
    groups = [[step] for step in steps]
    if by_partner:
        far = [4, 6, 2] if tiles == 8 else range(tiles - 2, 0, -2)
        groups = [[step, step + 1] for step in far] + [[1], [0]]
        steps = [step for group in groups for step in group]

    t_rows = t_slab.reshape(c_width * rows_i, full_width)

    def pack(some_groups, last):
        pairs = sum(len(group) for group in some_groups) // 2
        plan = (rows_i, run, c_width, by_partner, b_width // TILE, some_groups, steps * last)
        arguments = [k_irrep, i_irrep, tile_irrep, t_rows]
        shapes = [
            jax.ShapeDtypeStruct((len(group), deep, TILE), t_slab.dtype) for group in some_groups
        ]
        scratch = [
            small(k_irrep),
            small(i_irrep),
            small(tile_irrep),
            pltpu.VMEM((pairs, t_rows.shape[0], 2 * TILE), t_slab.dtype),
            pltpu.SemaphoreType.DMA((3 + last,)),
            pltpu.SemaphoreType.DMA((pairs,)),
        ]
        if last:
            arguments += [j_irrep, w_cycle.reshape(full_width, full_width)]
            shapes += [
                jax.ShapeDtypeStruct((TILE, full_width), w_cycle.dtype),
                jax.ShapeDtypeStruct((tiles, tiles, TILE), jnp.float32),
            ]
            scratch += [small(j_irrep), pltpu.SemaphoreType.DMA((tiles,))]
        return pl.pallas_call(
            lambda *refs: pack_kernel(plan, *refs),
            in_specs=[hbm()] * len(arguments),
            out_specs=[vmem()] * len(shapes),
            out_shape=shapes,
            scratch_shapes=scratch,
            compiler_params=limit(52 if last else 62),
            name="pack_near" if last else "pack_far",
        )(*arguments)

    packed = list(pack(groups[:3], False)) if by_partner else []
    *near, chosen_w, choice = pack(groups[len(packed) :], True)
    packed += near

    if by_partner:
        *far, beside, own = packed
        left = [swap(pair, "blk", group[0]) for pair, group in zip(far, groups)]
        left += [swap(beside, "blk", 1), own]
        left[2], left[-2], choice = lax.optimization_barrier((left[2], left[-2], choice))
        handed = []
        for pair in left[: len(far)]:
            block = pl.pallas_call(
                second_kernel,
                in_specs=[vmem()],
                out_specs=vmem(),
                out_shape=jax.ShapeDtypeStruct((1,) + pair.shape[1:], pair.dtype),
                compiler_params=limit(8),
                name="second",
            )(pair)
            handed.append(swap(block, "blk", 1))
        spots = []
        for n in range(len(far)):
            spots += [(n, 0), (len(left) + n, 0)]
        spots += [(len(far), 0), (len(far) + 1, 0)]
        left += handed
        part_shapes = [
            jax.ShapeDtypeStruct((wide + SPARE, b_width), jnp.bfloat16)
        ] * (rep_count - 1) + [jax.ShapeDtypeStruct((wide, b_width), jnp.float32)]
    else:
        stacked = jnp.concatenate(packed).reshape(tiles, c_width, run, TILE // a_width, a_width)
        outgoing = stacked.transpose(0, 3, 1, 2, 4).reshape(blk_count, c_width, wide)
        arrived = lax.all_to_all(outgoing, "blk", split_axis=0, concat_axis=0, tiled=True)
        left = [arrived.reshape(tiles, TILE, wide)]
        spots = [(0, n) for n in range(tiles)]
        part_shapes = [jax.ShapeDtypeStruct((wide, full_width), jnp.float32)]

    partials = pl.pallas_call(
        lambda *refs: multiply_kernel(spots, len(part_shapes), *refs),
        in_specs=[vmem()] * (2 + len(left)),
        out_specs=[vmem()] * len(part_shapes),
        out_shape=part_shapes,
        compiler_params=limit(16),
        name="multiply",
    )(chosen_w, choice, *left)

    out_shape = jax.ShapeDtypeStruct((rows_i, a_width, b_width), jnp.float32)
    denom, run_row, zeros = pl.pallas_call(
        lambda *refs: scale_kernel(a_width, *refs),
        in_specs=[hbm()] * 5 + [vmem(), pl.BlockSpec(memory_space=pl.ANY)],
        out_specs=[vmem(), vmem(), hbm()],
        out_shape=[
            jax.ShapeDtypeStruct((wide, b_width), jnp.float32),
            jax.ShapeDtypeStruct((8, b_width), jnp.float32),
            out_shape,
        ],
        scratch_shapes=[
            small(i_irrep),
            small(j_irrep),
            small(tile_irrep),
            small(i_energy),
            small(j_energy),
            pltpu.VMEM((TILE, TILE), jnp.float32),
            pltpu.VMEM((run, a_width, b_width), jnp.float32),
            pltpu.SemaphoreType.DMA((5,)),
            pltpu.SemaphoreType.DMA((tiles,)),
        ],
        compiler_params=limit(8),
        name="scale",
    )(
        i_irrep, j_irrep, tile_irrep, i_energy, j_energy,
        vir_energy.reshape(full_width // TILE, TILE), partials[-1],
    )

    if by_partner:
        gathered = [
            swap(part, "rep", rep_count - 1 - n) for n, part in enumerate(partials[:-1])
        ] + [partials[-1]]
        while len(gathered) > 2:
            first, *gathered, so_far = gathered
            added = pl.pallas_call(
                add_kernel,
                in_specs=[vmem()] * 2,
                out_specs=vmem(),
                out_shape=jax.ShapeDtypeStruct(so_far.shape, so_far.dtype),
                compiler_params=limit(8),
                name="add",
            )(first, so_far)
            gathered.append(added)
    else:
        outgoing = partials[0].reshape(wide, rep_count, b_width).transpose(1, 0, 2)
        arrived = lax.all_to_all(outgoing, "rep", split_axis=0, concat_axis=0, tiled=True)
        gathered = [arrived[n] for n in range(rep_count)]

    part_width = min(TILE, b_width)
    result = pl.pallas_call(
        lambda *refs: place_kernel(run, *refs),
        in_specs=[vmem(), vmem(), hbm()] + [vmem()] * len(gathered),
        out_specs=hbm(),
        out_shape=out_shape,
        input_output_aliases={2: 0},
        scratch_shapes=[
            pltpu.VMEM((b_width // part_width, run, a_width, part_width), jnp.float32),
            pltpu.SemaphoreType.DMA((b_width // part_width,)),
        ],
        compiler_params=limit(16),
        name="place",
    )(denom, run_row, zeros, *gathered)
    return result.reshape(rows_j, rows_i, a_width, b_width)


def solution(mesh):
    in_specs = (
        P("rep", "blk", None, None),
        P("rep", None, None, None),
        P("rep"),
        P(),
        P(),
        P(),
        P(),
        P(),
        P(),
    )
    out_specs = P(None, None, "blk", "rep")
    return jax.shard_map(shards, mesh=mesh, in_specs=in_specs, out_specs=out_specs, check_vma=False)
```

```python
import jax
import jax.numpy as jnp
from jax import lax
from jax.experimental import pallas as pl
from jax.experimental.pallas import tpu as pltpu
from jax.sharding import PartitionSpec as P

TILE = 128
CHUNK = 256
POWER = 17
TOP = 128.0
LEAST = 2.0**-100
SMALLEST = 2.0**-126
SPARE = 16


def vmem():
    return pl.BlockSpec(memory_space=pltpu.VMEM)


def hbm():
    return pl.BlockSpec(memory_space=pltpu.HBM)


def small(array):
    return pltpu.SMEM(array.shape, array.dtype)


def limit(mebibytes):
    return pltpu.CompilerParams(vmem_limit_bytes=mebibytes * 2**20)


def place_of(ref, stride, label):
    found = jnp.int32(0)
    for n in range(ref.shape[0] // stride):
        found = jnp.where(ref[n * stride] == label, jnp.int32(n), found)
    return found


def start_all(sources, targets, sems):
    copies = []
    for n, (source, target) in enumerate(zip(sources, targets)):
        copies.append(pltpu.make_async_copy(source, target, sems.at[n]))
        copies[-1].start()
    return copies


def pack_kernel(plan, *refs):
    rows_i, run, c_width, by_partner, tiles_b, groups, steps = plan
    if steps:
        k_hbm, i_hbm, tile_hbm, t_hbm, j_hbm, w_hbm, *refs = refs
        *refs, j_ref, w_sems = refs
    else:
        k_hbm, i_hbm, tile_hbm, t_hbm, *refs = refs
    *refs, k_ref, i_ref, tile_ref, t_ref, small_sems, t_sems = refs
    out_refs = refs[: len(groups)]
    runs = rows_i // run
    rows = CHUNK // runs
    sources, targets = [k_hbm, i_hbm, tile_hbm], [k_ref, i_ref, tile_ref]
    if steps:
        sources.append(j_hbm)
        targets.append(j_ref)
    small_copies = start_all(sources, targets, small_sems)
    me = lax.axis_index("blk") if by_partner else 0
    places = {
        step: (out_ref, spot)
        for out_ref, group in zip(out_refs, groups)
        for spot, step in enumerate(group)
    }
    pairs = [step for step in places if step % 2 == 0]
    columns = [
        pl.ds(pl.multiple_of(((me ^ step) | 1) * TILE - TILE, 2 * TILE), 2 * TILE)
        for step in pairs
    ]
    t_copies = start_all(
        [t_hbm.at[:, span] for span in columns],
        [t_ref.at[n] for n in range(len(pairs))],
        t_sems,
    )
    row = lax.broadcasted_iota(jnp.int32, (rows, CHUNK), 0)
    col = lax.broadcasted_iota(jnp.int32, (rows, CHUNK), 1)
    run_bits = run.bit_length() - 1
    same_c = (row >> run_bits) == (col >> (rows_i.bit_length() - 1))
    same_m = (row & (run - 1)) == (col & (run - 1))
    of_run = jnp.where(same_c & same_m, (col >> run_bits) & (runs - 1), -1)
    own_tile = lax.axis_index("blk") * c_width // TILE
    for copy in small_copies:
        copy.wait()
    w_copies = []
    if steps:
        w_ref, choice_ref = refs[len(groups) :]
        side = lax.axis_index("rep") * tiles_b if by_partner else 0
        flip = len(steps) - tiles_b if by_partner else 0
        label_w = k_ref[0] ^ j_ref[0]
        spot_row = lax.broadcasted_iota(jnp.int32, choice_ref.shape[1:], 0)
        for n in range(len(steps)):
            b_tile = n ^ flip ^ side
            c_tile = place_of(tile_ref, 1, label_w ^ tile_ref[b_tile])
            source = w_hbm.at[
                pl.ds(pl.multiple_of(c_tile * TILE, TILE), TILE),
                pl.ds(pl.multiple_of(b_tile * TILE, TILE), TILE),
            ]
            target = w_ref.at[:, pl.ds(n * TILE, TILE)]
            w_copies.append(pltpu.make_async_copy(source, target, w_sems.at[n]))
            w_copies[-1].start()
            spot = jnp.int32(0)
            for where, step in enumerate(steps):
                spot = jnp.where((c_tile ^ me) == step, jnp.int32(where), spot)
            choice_ref[n] = jnp.where(spot_row == spot, 1.0, 0.0)
    label = k_ref[0] ^ tile_ref[own_tile]
    picks = []
    for step in pairs:
        rows_of_pair = []
        for own in (step, step + 1):
            chosen = place_of(i_ref, run, label ^ tile_ref[me ^ own])
            rows_of_pair.append(jnp.where(of_run == chosen, 1.0, 0.0).astype(jnp.bfloat16))
        picks.append(jnp.concatenate(rows_of_pair, axis=0))
    swapped = (me & 1) == 1
    for n, step in enumerate(pairs):
        t_copies[n].wait()
        for chunk in range(t_ref.shape[1] // CHUNK):
            block = t_ref[n, chunk * CHUNK : (chunk + 1) * CHUNK, :]
            kept = jnp.dot(picks[n], block, preferred_element_type=jnp.float32)
            low, high = kept[:, :TILE], kept[:, TILE:]
            for own, here, other in ((step, low, high), (step + 1, high, low)):
                half = slice((own - step) * rows, (own - step + 1) * rows)
                out_ref, spot = places[own]
                value = jnp.where(swapped, other[half], here[half])
                out_ref[spot, chunk * rows : (chunk + 1) * rows, :] = value.astype(out_ref.dtype)
    for copy in w_copies:
        copy.wait()


def write_coded(out_ref, value):
    rows, width = value.shape
    largest = jnp.max(jnp.abs(value), axis=0, keepdims=True)
    exponent = jnp.ceil(jnp.log2(jnp.maximum(largest, LEAST)))
    scaled = value * (TOP * jnp.exp2(-exponent))
    power = scaled
    for _ in range(POWER.bit_length() - 1):
        power = power * power
    out_ref[:rows, :] = (power * scaled).astype(out_ref.dtype)
    out_ref[rows:, :] = jnp.broadcast_to(exponent, (SPARE, width)).astype(out_ref.dtype)


def read_coded(ref):
    rows = ref.shape[0] - SPARE
    power = ref[:rows, :].astype(jnp.float32)
    exponent = ref[rows:, :].astype(jnp.float32)[:1, :]
    size = jnp.exp2(jnp.log2(jnp.maximum(jnp.abs(power), SMALLEST)) * (1.0 / POWER))
    size = jnp.where(power < 0, -size, size) * (jnp.exp2(exponent) * (1.0 / TOP))
    return jnp.where(power == 0, 0.0, size)


def second_kernel(pair_ref, out_ref):
    out_ref[...] = pair_ref[1:]


def multiply_kernel(spots, out_count, w_ref, choice_ref, *refs):
    out_refs = refs[-out_count:]
    blocks = [refs[n][spot] for n, spot in spots]
    tiles = choice_ref.shape[0]
    each = tiles // out_count
    for n, out_ref in enumerate(out_refs):
        products = []
        for tile in range(n * each, (n + 1) * each):
            left = jnp.zeros_like(blocks[0])
            for spot, block in enumerate(blocks):
                left = jnp.where(choice_ref[tile, spot : spot + 1, :] > 0.5, block, left)
            products.append(
                lax.dot_general(
                    left,
                    w_ref[:, tile * TILE : (tile + 1) * TILE],
                    (((0,), (0,)), ((), ())),
                    preferred_element_type=jnp.float32,
                )
            )
        value = jnp.concatenate(products, axis=1)
        if out_ref.dtype == jnp.float32:
            out_ref[...] = value
        else:
            write_coded(out_ref, value)


def scale_kernel(
    a_width, i_hbm, j_hbm, tile_hbm, ei_hbm, ej_hbm, ev_ref, after_hbm, denom_ref, run_ref,
    zero_hbm, i_ref, j_ref, tile_ref, ei_ref, ej_ref, column_ref, zero_ref, sems, zero_sems,
):
    copies = start_all(
        (i_hbm, j_hbm, tile_hbm, ei_hbm, ej_hbm), (i_ref, j_ref, tile_ref, ei_ref, ej_ref), sems
    )
    rows_i, b_width = i_ref.shape[0], run_ref.shape[1]
    run = rows_i // tile_ref.shape[0]
    zero_ref[...] = jnp.zeros_like(zero_ref)
    count = zero_ref.shape[0]
    zero_copies = start_all(
        [zero_ref] * (rows_i // count),
        [zero_hbm.at[pl.ds(n * count, count)] for n in range(rows_i // count)],
        zero_sems,
    )
    a_start = lax.axis_index("blk") * a_width
    b_start = lax.axis_index("rep") * b_width
    a_tile = a_start // TILE
    column_ref[...] = jnp.broadcast_to(ev_ref[pl.ds(a_tile, 1), :], (TILE, TILE)).T
    a_energy = column_ref[pl.ds(pl.multiple_of(a_start % TILE, a_width), a_width), :]
    width = min(TILE, b_width)
    for copy in copies:
        copy.wait()
    for part in range(b_width // width):
        b_tile = b_start // TILE + part
        b_tile_row = ev_ref[pl.ds(b_tile, 1), :]
        b_row = b_tile_row[:, :width]
        for n in range(1, TILE // width):
            piece = b_tile_row[:, n * width : (n + 1) * width]
            b_row = jnp.where(b_start % TILE == n * width, piece, b_row)
        chosen = place_of(i_ref, run, j_ref[0] ^ tile_ref[a_tile] ^ tile_ref[b_tile])
        columns = slice(part * width, (part + 1) * width)
        run_ref[:, columns] = jnp.full((run_ref.shape[0], width), chosen.astype(jnp.float32))
        sum_ab = a_energy[:, :width] + b_row
        for m in range(run):
            denom_ref[m * a_width : (m + 1) * a_width, columns] = (
                sum_ab - ei_ref[chosen * run + m] - ej_ref[0]
            )
    for copy in zero_copies:
        copy.wait()


def add_kernel(part_ref, so_far_ref, out_ref):
    out_ref[...] = so_far_ref[...] + read_coded(part_ref)


def place_kernel(run, denom_ref, run_ref, zero_hbm, *refs):
    parts_refs, out_hbm, block_ref, sems = refs[:-3], refs[-3], refs[-2], refs[-1]
    a_width, width = block_ref.shape[2:]
    spans = [slice(n * width, (n + 1) * width) for n in range(block_ref.shape[0])]
    chosen_runs = [jnp.max(run_ref[:, columns]).astype(jnp.int32) for columns in spans]
    total = parts_refs[-1][...]
    for parts_ref in parts_refs[:-1]:
        coded = parts_ref.dtype != jnp.float32
        total = total + (read_coded(parts_ref) if coded else parts_ref[...])
    scaled = total / denom_ref[...]
    copies = []
    for part, (columns, chosen) in enumerate(zip(spans, chosen_runs)):
        for m in range(run):
            block_ref[part, m] = scaled[m * a_width : (m + 1) * a_width, columns]
        target = out_hbm.at[pl.ds(chosen * run, run), :, pl.ds(part * width, width)]
        copies.append(pltpu.make_async_copy(block_ref.at[part], target, sems.at[part]))
        copies[-1].start()
    for copy in copies:
        copy.wait()


def swap(block, axis, step):
    return lax.ppermute(block, axis, [(n, n ^ step) for n in range(lax.axis_size(axis))])


def shards(t_slab, w_cycle, k_irrep, i_irrep, j_irrep, tile_irrep, i_energy, j_energy, vir_energy):
    blk_count = lax.axis_size("blk")
    rep_count = lax.axis_size("rep")
    k_rows, c_width, rows_i, full_width = t_slab.shape
    rows_j = w_cycle.shape[1]
    assert k_rows == 1 and rows_j == 1
    tiles = tile_irrep.shape[0]
    run = rows_i // tiles
    a_width = full_width // blk_count
    b_width = full_width // rep_count
    deep = c_width * run
    wide = run * a_width
    by_partner = a_width == TILE and b_width % TILE == 0 and run == 1
    steps = list(reversed(range(tiles))) if by_partner else list(range(tiles))
    groups = [[step] for step in steps]
    if by_partner:
        far = [4, 6, 2] if tiles == 8 else range(tiles - 2, 0, -2)
        groups = [[step, step + 1] for step in far] + [[1], [0]]
        steps = [step for group in groups for step in group]

    t_rows = t_slab.reshape(c_width * rows_i, full_width)

    def pack(some_groups, last):
        pairs = sum(len(group) for group in some_groups) // 2
        plan = (rows_i, run, c_width, by_partner, b_width // TILE, some_groups, steps * last)
        arguments = [k_irrep, i_irrep, tile_irrep, t_rows]
        shapes = [
            jax.ShapeDtypeStruct((len(group), deep, TILE), t_slab.dtype) for group in some_groups
        ]
        scratch = [
            small(k_irrep),
            small(i_irrep),
            small(tile_irrep),
            pltpu.VMEM((pairs, t_rows.shape[0], 2 * TILE), t_slab.dtype),
            pltpu.SemaphoreType.DMA((3 + last,)),
            pltpu.SemaphoreType.DMA((pairs,)),
        ]
        if last:
            arguments += [j_irrep, w_cycle.reshape(full_width, full_width)]
            shapes += [
                jax.ShapeDtypeStruct((TILE, full_width), w_cycle.dtype),
                jax.ShapeDtypeStruct((tiles, tiles, TILE), jnp.float32),
            ]
            scratch += [small(j_irrep), pltpu.SemaphoreType.DMA((tiles,))]
        return pl.pallas_call(
            lambda *refs: pack_kernel(plan, *refs),
            in_specs=[hbm()] * len(arguments),
            out_specs=[vmem()] * len(shapes),
            out_shape=shapes,
            scratch_shapes=scratch,
            compiler_params=limit(52 if last else 62),
            name="pack_near" if last else "pack_far",
        )(*arguments)

    packed = list(pack(groups[:3], False)) if by_partner else []
    *near, chosen_w, choice = pack(groups[len(packed) :], True)
    packed += near

    if by_partner:
        *far, beside, own = packed
        left = [swap(pair, "blk", group[0]) for pair, group in zip(far, groups)]
        left += [swap(beside, "blk", 1), own]
        left[2], left[-2], choice = lax.optimization_barrier((left[2], left[-2], choice))
        handed = []
        for pair in left[: len(far)]:
            block = pl.pallas_call(
                second_kernel,
                in_specs=[vmem()],
                out_specs=vmem(),
                out_shape=jax.ShapeDtypeStruct((1,) + pair.shape[1:], pair.dtype),
                compiler_params=limit(8),
                name="second",
            )(pair)
            handed.append(swap(block, "blk", 1))
        spots = []
        for n in range(len(far)):
            spots += [(n, 0), (len(left) + n, 0)]
        spots += [(len(far), 0), (len(far) + 1, 0)]
        left += handed
        part_shapes = [
            jax.ShapeDtypeStruct((wide + SPARE, b_width), jnp.bfloat16)
        ] * (rep_count - 1) + [jax.ShapeDtypeStruct((wide, b_width), jnp.float32)]
    else:
        stacked = jnp.concatenate(packed).reshape(tiles, c_width, run, TILE // a_width, a_width)
        outgoing = stacked.transpose(0, 3, 1, 2, 4).reshape(blk_count, c_width, wide)
        arrived = lax.all_to_all(outgoing, "blk", split_axis=0, concat_axis=0, tiled=True)
        left = [arrived.reshape(tiles, TILE, wide)]
        spots = [(0, n) for n in range(tiles)]
        part_shapes = [jax.ShapeDtypeStruct((wide, full_width), jnp.float32)]

    partials = pl.pallas_call(
        lambda *refs: multiply_kernel(spots, len(part_shapes), *refs),
        in_specs=[vmem()] * (2 + len(left)),
        out_specs=[vmem()] * len(part_shapes),
        out_shape=part_shapes,
        compiler_params=limit(16),
        name="multiply",
    )(chosen_w, choice, *left)

    out_shape = jax.ShapeDtypeStruct((rows_i, a_width, b_width), jnp.float32)
    denom, run_row, zeros = pl.pallas_call(
        lambda *refs: scale_kernel(a_width, *refs),
        in_specs=[hbm()] * 5 + [vmem(), pl.BlockSpec(memory_space=pl.ANY)],
        out_specs=[vmem(), vmem(), hbm()],
        out_shape=[
            jax.ShapeDtypeStruct((wide, b_width), jnp.float32),
            jax.ShapeDtypeStruct((8, b_width), jnp.float32),
            out_shape,
        ],
        scratch_shapes=[
            small(i_irrep),
            small(j_irrep),
            small(tile_irrep),
            small(i_energy),
            small(j_energy),
            pltpu.VMEM((TILE, TILE), jnp.float32),
            pltpu.VMEM((run, a_width, b_width), jnp.float32),
            pltpu.SemaphoreType.DMA((5,)),
            pltpu.SemaphoreType.DMA((tiles,)),
        ],
        compiler_params=limit(8),
        name="scale",
    )(
        i_irrep, j_irrep, tile_irrep, i_energy, j_energy,
        vir_energy.reshape(full_width // TILE, TILE), partials[-1],
    )

    if by_partner:
        gathered = [
            swap(part, "rep", rep_count - 1 - n) for n, part in enumerate(partials[:-1])
        ] + [partials[-1]]
        while len(gathered) > 2:
            first, *gathered, so_far = gathered
            added = pl.pallas_call(
                add_kernel,
                in_specs=[vmem()] * 2,
                out_specs=vmem(),
                out_shape=jax.ShapeDtypeStruct(so_far.shape, so_far.dtype),
                compiler_params=limit(8),
                name="add",
            )(first, so_far)
            gathered.append(added)
    else:
        outgoing = partials[0].reshape(wide, rep_count, b_width).transpose(1, 0, 2)
        arrived = lax.all_to_all(outgoing, "rep", split_axis=0, concat_axis=0, tiled=True)
        gathered = [arrived[n] for n in range(rep_count)]

    part_width = min(TILE, b_width)
    result = pl.pallas_call(
        lambda *refs: place_kernel(run, *refs),
        in_specs=[vmem(), vmem(), hbm()] + [vmem()] * len(gathered),
        out_specs=hbm(),
        out_shape=out_shape,
        input_output_aliases={2: 0},
        scratch_shapes=[
            pltpu.VMEM((b_width // part_width, run, a_width, part_width), jnp.float32),
            pltpu.SemaphoreType.DMA((b_width // part_width,)),
        ],
        compiler_params=limit(16),
        name="place",
    )(denom, run_row, zeros, *gathered)
    return result.reshape(rows_j, rows_i, a_width, b_width)


def solution(mesh):
    in_specs = (
        P("rep", "blk", None, None),
        P("rep", None, None, None),
        P("rep"),
        P(),
        P(),
        P(),
        P(),
        P(),
        P(),
    )
    out_specs = P(None, None, "blk", "rep")
    return jax.shard_map(shards, mesh=mesh, in_specs=in_specs, out_specs=out_specs, check_vma=False)
```

```python
import jax
import jax.numpy as jnp
from jax import lax
from jax.experimental import pallas as pl
from jax.experimental.pallas import tpu as pltpu
from jax.sharding import PartitionSpec as P

TILE = 128
CHUNK = 256
POWER = 17
TOP = 128.0
ABOVE = 1.01
LEAST = 2.0**-100
SMALLEST = 2.0**-126
SPARE = 16


def vmem():
    return pl.BlockSpec(memory_space=pltpu.VMEM)


def hbm():
    return pl.BlockSpec(memory_space=pltpu.HBM)


def small(array):
    return pltpu.SMEM(array.shape, array.dtype)


def limit(mebibytes):
    return pltpu.CompilerParams(vmem_limit_bytes=mebibytes * 2**20)


def place_of(ref, stride, label):
    found = jnp.int32(0)
    for n in range(ref.shape[0] // stride):
        found = jnp.where(ref[n * stride] == label, jnp.int32(n), found)
    return found


def start_all(sources, targets, sems):
    copies = []
    for n, (source, target) in enumerate(zip(sources, targets)):
        copies.append(pltpu.make_async_copy(source, target, sems.at[n]))
        copies[-1].start()
    return copies


def pack_kernel(plan, *refs):
    rows_i, run, c_width, by_partner, tiles_b, groups, steps = plan
    if steps:
        k_hbm, i_hbm, tile_hbm, t_hbm, j_hbm, w_hbm, *refs = refs
        *refs, j_ref, w_sems = refs
    else:
        k_hbm, i_hbm, tile_hbm, t_hbm, *refs = refs
    *refs, k_ref, i_ref, tile_ref, t_ref, small_sems, t_sems = refs
    out_refs = refs[: len(groups)]
    runs = rows_i // run
    rows = CHUNK // runs
    sources, targets = [k_hbm, i_hbm, tile_hbm], [k_ref, i_ref, tile_ref]
    if steps:
        sources.append(j_hbm)
        targets.append(j_ref)
    small_copies = start_all(sources, targets, small_sems)
    me = lax.axis_index("blk") if by_partner else 0
    places = {
        step: (out_ref, spot)
        for out_ref, group in zip(out_refs, groups)
        for spot, step in enumerate(group)
    }
    pairs = [step for step in places if step % 2 == 0]
    columns = [
        pl.ds(pl.multiple_of(((me ^ step) | 1) * TILE - TILE, 2 * TILE), 2 * TILE)
        for step in pairs
    ]
    t_copies = start_all(
        [t_hbm.at[:, span] for span in columns],
        [t_ref.at[n] for n in range(len(pairs))],
        t_sems,
    )
    row = lax.broadcasted_iota(jnp.int32, (rows, CHUNK), 0)
    col = lax.broadcasted_iota(jnp.int32, (rows, CHUNK), 1)
    run_bits = run.bit_length() - 1
    same_c = (row >> run_bits) == (col >> (rows_i.bit_length() - 1))
    same_m = (row & (run - 1)) == (col & (run - 1))
    of_run = jnp.where(same_c & same_m, (col >> run_bits) & (runs - 1), -1)
    own_tile = lax.axis_index("blk") * c_width // TILE
    for copy in small_copies:
        copy.wait()
    w_copies = []
    if steps:
        w_ref, choice_ref = refs[len(groups) :]
        side = lax.axis_index("rep") * tiles_b if by_partner else 0
        flip = len(steps) - tiles_b if by_partner else 0
        label_w = k_ref[0] ^ j_ref[0]
        spot_row = lax.broadcasted_iota(jnp.int32, choice_ref.shape[1:], 0)
        for n in range(len(steps)):
            b_tile = n ^ flip ^ side
            c_tile = place_of(tile_ref, 1, label_w ^ tile_ref[b_tile])
            source = w_hbm.at[
                pl.ds(pl.multiple_of(c_tile * TILE, TILE), TILE),
                pl.ds(pl.multiple_of(b_tile * TILE, TILE), TILE),
            ]
            target = w_ref.at[:, pl.ds(n * TILE, TILE)]
            w_copies.append(pltpu.make_async_copy(source, target, w_sems.at[n]))
            w_copies[-1].start()
            spot = jnp.int32(0)
            for where, step in enumerate(steps):
                spot = jnp.where((c_tile ^ me) == step, jnp.int32(where), spot)
            choice_ref[n] = jnp.where(spot_row == spot, 1.0, 0.0)
    label = k_ref[0] ^ tile_ref[own_tile]
    picks = []
    for step in pairs:
        rows_of_pair = []
        for own in (step, step + 1):
            chosen = place_of(i_ref, run, label ^ tile_ref[me ^ own])
            rows_of_pair.append(jnp.where(of_run == chosen, 1.0, 0.0).astype(jnp.bfloat16))
        picks.append(jnp.concatenate(rows_of_pair, axis=0))
    swapped = (me & 1) == 1
    for n, step in enumerate(pairs):
        t_copies[n].wait()
        for chunk in range(t_ref.shape[1] // CHUNK):
            block = t_ref[n, chunk * CHUNK : (chunk + 1) * CHUNK, :]
            kept = jnp.dot(picks[n], block, preferred_element_type=jnp.float32)
            low, high = kept[:, :TILE], kept[:, TILE:]
            for own, here, other in ((step, low, high), (step + 1, high, low)):
                half = slice((own - step) * rows, (own - step + 1) * rows)
                out_ref, spot = places[own]
                value = jnp.where(swapped, other[half], here[half])
                out_ref[spot, chunk * rows : (chunk + 1) * rows, :] = value.astype(out_ref.dtype)
    for copy in w_copies:
        copy.wait()


def write_coded(out_ref, value):
    rows, width = value.shape
    largest = jnp.max(jnp.abs(value), axis=0, keepdims=True)
    scale = jnp.maximum(largest * ABOVE, LEAST).astype(out_ref.dtype)
    scaled = value * (TOP / scale.astype(jnp.float32))
    power = scaled
    for _ in range(POWER.bit_length() - 1):
        power = power * power
    out_ref[:rows, :] = (power * scaled).astype(out_ref.dtype)
    out_ref[rows:, :] = jnp.broadcast_to(scale, (SPARE, width))


def read_coded(ref):
    rows = ref.shape[0] - SPARE
    power = ref[:rows, :].astype(jnp.float32)
    scale = ref[rows:, :].astype(jnp.float32)[:1, :]
    size = jnp.exp2(jnp.log2(jnp.maximum(jnp.abs(power), SMALLEST)) * (1.0 / POWER))
    size = jnp.where(power < 0, -size, size) * (scale * (1.0 / TOP))
    return jnp.where(power == 0, 0.0, size)


def second_kernel(pair_ref, out_ref):
    out_ref[...] = pair_ref[1:]


def multiply_kernel(spots, out_count, w_ref, choice_ref, *refs):
    out_refs = refs[-out_count:]
    blocks = [refs[n][spot] for n, spot in spots]
    tiles = choice_ref.shape[0]
    each = tiles // out_count
    for n, out_ref in enumerate(out_refs):
        products = []
        for tile in range(n * each, (n + 1) * each):
            left = jnp.zeros_like(blocks[0])
            for spot, block in enumerate(blocks):
                left = jnp.where(choice_ref[tile, spot : spot + 1, :] > 0.5, block, left)
            products.append(
                lax.dot_general(
                    left,
                    w_ref[:, tile * TILE : (tile + 1) * TILE],
                    (((0,), (0,)), ((), ())),
                    preferred_element_type=jnp.float32,
                )
            )
        value = jnp.concatenate(products, axis=1)
        if out_ref.dtype == jnp.float32:
            out_ref[...] = value
        else:
            write_coded(out_ref, value)


def scale_kernel(
    a_width, i_hbm, j_hbm, tile_hbm, ei_hbm, ej_hbm, ev_ref, after_hbm, denom_ref, run_ref,
    zero_hbm, i_ref, j_ref, tile_ref, ei_ref, ej_ref, column_ref, zero_ref, sems, zero_sems,
):
    copies = start_all(
        (i_hbm, j_hbm, tile_hbm, ei_hbm, ej_hbm), (i_ref, j_ref, tile_ref, ei_ref, ej_ref), sems
    )
    rows_i, b_width = i_ref.shape[0], run_ref.shape[1]
    run = rows_i // tile_ref.shape[0]
    zero_ref[...] = jnp.zeros_like(zero_ref)
    count = zero_ref.shape[0]
    zero_copies = start_all(
        [zero_ref] * (rows_i // count),
        [zero_hbm.at[pl.ds(n * count, count)] for n in range(rows_i // count)],
        zero_sems,
    )
    a_start = lax.axis_index("blk") * a_width
    b_start = lax.axis_index("rep") * b_width
    a_tile = a_start // TILE
    column_ref[...] = jnp.broadcast_to(ev_ref[pl.ds(a_tile, 1), :], (TILE, TILE)).T
    a_energy = column_ref[pl.ds(pl.multiple_of(a_start % TILE, a_width), a_width), :]
    width = min(TILE, b_width)
    for copy in copies:
        copy.wait()
    for part in range(b_width // width):
        b_tile = b_start // TILE + part
        b_tile_row = ev_ref[pl.ds(b_tile, 1), :]
        b_row = b_tile_row[:, :width]
        for n in range(1, TILE // width):
            piece = b_tile_row[:, n * width : (n + 1) * width]
            b_row = jnp.where(b_start % TILE == n * width, piece, b_row)
        chosen = place_of(i_ref, run, j_ref[0] ^ tile_ref[a_tile] ^ tile_ref[b_tile])
        columns = slice(part * width, (part + 1) * width)
        run_ref[:, columns] = jnp.full((run_ref.shape[0], width), chosen.astype(jnp.float32))
        sum_ab = a_energy[:, :width] + b_row
        for m in range(run):
            denom_ref[m * a_width : (m + 1) * a_width, columns] = (
                sum_ab - ei_ref[chosen * run + m] - ej_ref[0]
            )
    for copy in zero_copies:
        copy.wait()


def add_kernel(part_ref, so_far_ref, out_ref):
    out_ref[...] = so_far_ref[...] + read_coded(part_ref)


def place_kernel(run, denom_ref, run_ref, zero_hbm, *refs):
    parts_refs, out_hbm, block_ref, sems = refs[:-3], refs[-3], refs[-2], refs[-1]
    a_width, width = block_ref.shape[2:]
    spans = [slice(n * width, (n + 1) * width) for n in range(block_ref.shape[0])]
    chosen_runs = [jnp.max(run_ref[:, columns]).astype(jnp.int32) for columns in spans]
    total = parts_refs[-1][...]
    for parts_ref in parts_refs[:-1]:
        coded = parts_ref.dtype != jnp.float32
        total = total + (read_coded(parts_ref) if coded else parts_ref[...])
    scaled = total / denom_ref[...]
    copies = []
    for part, (columns, chosen) in enumerate(zip(spans, chosen_runs)):
        for m in range(run):
            block_ref[part, m] = scaled[m * a_width : (m + 1) * a_width, columns]
        target = out_hbm.at[pl.ds(chosen * run, run), :, pl.ds(part * width, width)]
        copies.append(pltpu.make_async_copy(block_ref.at[part], target, sems.at[part]))
        copies[-1].start()
    for copy in copies:
        copy.wait()


def swap(block, axis, step):
    return lax.ppermute(block, axis, [(n, n ^ step) for n in range(lax.axis_size(axis))])


def shards(t_slab, w_cycle, k_irrep, i_irrep, j_irrep, tile_irrep, i_energy, j_energy, vir_energy):
    blk_count = lax.axis_size("blk")
    rep_count = lax.axis_size("rep")
    k_rows, c_width, rows_i, full_width = t_slab.shape
    rows_j = w_cycle.shape[1]
    assert k_rows == 1 and rows_j == 1
    tiles = tile_irrep.shape[0]
    run = rows_i // tiles
    a_width = full_width // blk_count
    b_width = full_width // rep_count
    deep = c_width * run
    wide = run * a_width
    by_partner = a_width == TILE and b_width % TILE == 0 and run == 1
    steps = list(reversed(range(tiles))) if by_partner else list(range(tiles))
    groups = [[step] for step in steps]
    if by_partner:
        far = [4, 6, 2] if tiles == 8 else range(tiles - 2, 0, -2)
        groups = [[step, step + 1] for step in far] + [[1], [0]]
        steps = [step for group in groups for step in group]

    t_rows = t_slab.reshape(c_width * rows_i, full_width)

    def pack(some_groups, last):
        pairs = sum(len(group) for group in some_groups) // 2
        plan = (rows_i, run, c_width, by_partner, b_width // TILE, some_groups, steps * last)
        arguments = [k_irrep, i_irrep, tile_irrep, t_rows]
        shapes = [
            jax.ShapeDtypeStruct((len(group), deep, TILE), t_slab.dtype) for group in some_groups
        ]
        scratch = [
            small(k_irrep),
            small(i_irrep),
            small(tile_irrep),
            pltpu.VMEM((pairs, t_rows.shape[0], 2 * TILE), t_slab.dtype),
            pltpu.SemaphoreType.DMA((3 + last,)),
            pltpu.SemaphoreType.DMA((pairs,)),
        ]
        if last:
            arguments += [j_irrep, w_cycle.reshape(full_width, full_width)]
            shapes += [
                jax.ShapeDtypeStruct((TILE, full_width), w_cycle.dtype),
                jax.ShapeDtypeStruct((tiles, tiles, TILE), jnp.float32),
            ]
            scratch += [small(j_irrep), pltpu.SemaphoreType.DMA((tiles,))]
        return pl.pallas_call(
            lambda *refs: pack_kernel(plan, *refs),
            in_specs=[hbm()] * len(arguments),
            out_specs=[vmem()] * len(shapes),
            out_shape=shapes,
            scratch_shapes=scratch,
            compiler_params=limit(52 if last else 62),
            name="pack_near" if last else "pack_far",
        )(*arguments)

    packed = list(pack(groups[:3], False)) if by_partner else []
    *near, chosen_w, choice = pack(groups[len(packed) :], True)
    packed += near

    if by_partner:
        *far, beside, own = packed
        left = [swap(pair, "blk", group[0]) for pair, group in zip(far, groups)]
        left += [swap(beside, "blk", 1), own]
        left[2], left[-2], choice = lax.optimization_barrier((left[2], left[-2], choice))
        handed = []
        for pair in left[: len(far)]:
            block = pl.pallas_call(
                second_kernel,
                in_specs=[vmem()],
                out_specs=vmem(),
                out_shape=jax.ShapeDtypeStruct((1,) + pair.shape[1:], pair.dtype),
                compiler_params=limit(8),
                name="second",
            )(pair)
            handed.append(swap(block, "blk", 1))
        spots = []
        for n in range(len(far)):
            spots += [(n, 0), (len(left) + n, 0)]
        spots += [(len(far), 0), (len(far) + 1, 0)]
        left += handed
        part_shapes = [
            jax.ShapeDtypeStruct((wide + SPARE, b_width), jnp.bfloat16)
        ] * (rep_count - 1) + [jax.ShapeDtypeStruct((wide, b_width), jnp.float32)]
    else:
        stacked = jnp.concatenate(packed).reshape(tiles, c_width, run, TILE // a_width, a_width)
        outgoing = stacked.transpose(0, 3, 1, 2, 4).reshape(blk_count, c_width, wide)
        arrived = lax.all_to_all(outgoing, "blk", split_axis=0, concat_axis=0, tiled=True)
        left = [arrived.reshape(tiles, TILE, wide)]
        spots = [(0, n) for n in range(tiles)]
        part_shapes = [jax.ShapeDtypeStruct((wide, full_width), jnp.float32)]

    partials = pl.pallas_call(
        lambda *refs: multiply_kernel(spots, len(part_shapes), *refs),
        in_specs=[vmem()] * (2 + len(left)),
        out_specs=[vmem()] * len(part_shapes),
        out_shape=part_shapes,
        compiler_params=limit(16),
        name="multiply",
    )(chosen_w, choice, *left)

    out_shape = jax.ShapeDtypeStruct((rows_i, a_width, b_width), jnp.float32)
    denom, run_row, zeros = pl.pallas_call(
        lambda *refs: scale_kernel(a_width, *refs),
        in_specs=[hbm()] * 5 + [vmem(), pl.BlockSpec(memory_space=pl.ANY)],
        out_specs=[vmem(), vmem(), hbm()],
        out_shape=[
            jax.ShapeDtypeStruct((wide, b_width), jnp.float32),
            jax.ShapeDtypeStruct((8, b_width), jnp.float32),
            out_shape,
        ],
        scratch_shapes=[
            small(i_irrep),
            small(j_irrep),
            small(tile_irrep),
            small(i_energy),
            small(j_energy),
            pltpu.VMEM((TILE, TILE), jnp.float32),
            pltpu.VMEM((run, a_width, b_width), jnp.float32),
            pltpu.SemaphoreType.DMA((5,)),
            pltpu.SemaphoreType.DMA((tiles,)),
        ],
        compiler_params=limit(8),
        name="scale",
    )(
        i_irrep, j_irrep, tile_irrep, i_energy, j_energy,
        vir_energy.reshape(full_width // TILE, TILE), partials[-1],
    )

    if by_partner:
        gathered = [
            swap(part, "rep", rep_count - 1 - n) for n, part in enumerate(partials[:-1])
        ] + [partials[-1]]
        while len(gathered) > 2:
            first, *gathered, so_far = gathered
            added = pl.pallas_call(
                add_kernel,
                in_specs=[vmem()] * 2,
                out_specs=vmem(),
                out_shape=jax.ShapeDtypeStruct(so_far.shape, so_far.dtype),
                compiler_params=limit(8),
                name="add",
            )(first, so_far)
            gathered.append(added)
    else:
        outgoing = partials[0].reshape(wide, rep_count, b_width).transpose(1, 0, 2)
        arrived = lax.all_to_all(outgoing, "rep", split_axis=0, concat_axis=0, tiled=True)
        gathered = [arrived[n] for n in range(rep_count)]

    part_width = min(TILE, b_width)
    result = pl.pallas_call(
        lambda *refs: place_kernel(run, *refs),
        in_specs=[vmem(), vmem(), hbm()] + [vmem()] * len(gathered),
        out_specs=hbm(),
        out_shape=out_shape,
        input_output_aliases={2: 0},
        scratch_shapes=[
            pltpu.VMEM((b_width // part_width, run, a_width, part_width), jnp.float32),
            pltpu.SemaphoreType.DMA((b_width // part_width,)),
        ],
        compiler_params=limit(16),
        name="place",
    )(denom, run_row, zeros, *gathered)
    return result.reshape(rows_j, rows_i, a_width, b_width)


def solution(mesh):
    in_specs = (
        P("rep", "blk", None, None),
        P("rep", None, None, None),
        P("rep"),
        P(),
        P(),
        P(),
        P(),
        P(),
        P(),
    )
    out_specs = P(None, None, "blk", "rep")
    return jax.shard_map(shards, mesh=mesh, in_specs=in_specs, out_specs=out_specs, check_vma=False)
```

```python
import jax
import jax.numpy as jnp
from jax import lax
from jax.experimental import pallas as pl
from jax.experimental.pallas import tpu as pltpu
from jax.sharding import PartitionSpec as P

TILE = 128
CHUNK = 256
POWER = 17
TOP = 128.0
LEAST = 2.0**-100
SMALLEST = 2.0**-126
SPARE = 16


def vmem():
    return pl.BlockSpec(memory_space=pltpu.VMEM)


def hbm():
    return pl.BlockSpec(memory_space=pltpu.HBM)


def small(array):
    return pltpu.SMEM(array.shape, array.dtype)


def limit(mebibytes):
    return pltpu.CompilerParams(vmem_limit_bytes=mebibytes * 2**20)


def place_of(ref, stride, label):
    found = jnp.int32(0)
    for n in range(ref.shape[0] // stride):
        found = jnp.where(ref[n * stride] == label, jnp.int32(n), found)
    return found


def start_all(sources, targets, sems):
    copies = []
    for n, (source, target) in enumerate(zip(sources, targets)):
        copies.append(pltpu.make_async_copy(source, target, sems.at[n]))
        copies[-1].start()
    return copies


def pack_kernel(plan, *refs):
    rows_i, run, c_width, by_partner, tiles_b, groups, steps = plan
    if steps:
        k_hbm, i_hbm, tile_hbm, t_hbm, j_hbm, w_hbm, *refs = refs
        *refs, j_ref, w_sems = refs
    else:
        k_hbm, i_hbm, tile_hbm, t_hbm, *refs = refs
    *refs, k_ref, i_ref, tile_ref, t_ref, small_sems, t_sems = refs
    out_refs = refs[: len(groups)]
    runs = rows_i // run
    rows = CHUNK // runs
    sources, targets = [k_hbm, i_hbm, tile_hbm], [k_ref, i_ref, tile_ref]
    if steps:
        sources.append(j_hbm)
        targets.append(j_ref)
    small_copies = start_all(sources, targets, small_sems)
    me = lax.axis_index("blk") if by_partner else 0
    places = {
        step: (out_ref, spot)
        for out_ref, group in zip(out_refs, groups)
        for spot, step in enumerate(group)
    }
    pairs = [step for step in places if step % 2 == 0]
    columns = [
        pl.ds(pl.multiple_of(((me ^ step) | 1) * TILE - TILE, 2 * TILE), 2 * TILE)
        for step in pairs
    ]
    t_copies = start_all(
        [t_hbm.at[:, span] for span in columns],
        [t_ref.at[n] for n in range(len(pairs))],
        t_sems,
    )
    row = lax.broadcasted_iota(jnp.int32, (rows, CHUNK), 0)
    col = lax.broadcasted_iota(jnp.int32, (rows, CHUNK), 1)
    run_bits = run.bit_length() - 1
    same_c = (row >> run_bits) == (col >> (rows_i.bit_length() - 1))
    same_m = (row & (run - 1)) == (col & (run - 1))
    of_run = jnp.where(same_c & same_m, (col >> run_bits) & (runs - 1), -1)
    own_tile = lax.axis_index("blk") * c_width // TILE
    for copy in small_copies:
        copy.wait()
    w_copies = []
    if steps:
        w_ref, choice_ref = refs[len(groups) :]
        side = lax.axis_index("rep") * tiles_b if by_partner else 0
        flip = len(steps) - tiles_b if by_partner else 0
        label_w = k_ref[0] ^ j_ref[0]
        spot_row = lax.broadcasted_iota(jnp.int32, choice_ref.shape[1:], 0)
        for n in range(len(steps)):
            b_tile = n ^ flip ^ side
            c_tile = place_of(tile_ref, 1, label_w ^ tile_ref[b_tile])
            source = w_hbm.at[
                pl.ds(pl.multiple_of(c_tile * TILE, TILE), TILE),
                pl.ds(pl.multiple_of(b_tile * TILE, TILE), TILE),
            ]
            target = w_ref.at[:, pl.ds(n * TILE, TILE)]
            w_copies.append(pltpu.make_async_copy(source, target, w_sems.at[n]))
            w_copies[-1].start()
            spot = jnp.int32(0)
            for where, step in enumerate(steps):
                spot = jnp.where((c_tile ^ me) == step, jnp.int32(where), spot)
            choice_ref[n] = jnp.where(spot_row == spot, 1.0, 0.0)
    label = k_ref[0] ^ tile_ref[own_tile]
    picks = []
    for step in pairs:
        rows_of_pair = []
        for own in (step, step + 1):
            chosen = place_of(i_ref, run, label ^ tile_ref[me ^ own])
            rows_of_pair.append(jnp.where(of_run == chosen, 1.0, 0.0).astype(jnp.bfloat16))
        picks.append(jnp.concatenate(rows_of_pair, axis=0))
    swapped = (me & 1) == 1
    for n, step in enumerate(pairs):
        t_copies[n].wait()
        for chunk in range(t_ref.shape[1] // CHUNK):
            block = t_ref[n, chunk * CHUNK : (chunk + 1) * CHUNK, :]
            kept = jnp.dot(picks[n], block, preferred_element_type=jnp.float32)
            low, high = kept[:, :TILE], kept[:, TILE:]
            for own, here, other in ((step, low, high), (step + 1, high, low)):
                half = slice((own - step) * rows, (own - step + 1) * rows)
                out_ref, spot = places[own]
                value = jnp.where(swapped, other[half], here[half])
                out_ref[spot, chunk * rows : (chunk + 1) * rows, :] = value.astype(out_ref.dtype)
    for copy in w_copies:
        copy.wait()


def write_coded(out_ref, value):
    rows, width = value.shape
    largest = jnp.max(jnp.abs(value), axis=0, keepdims=True)
    exponent = jnp.ceil(jnp.log2(jnp.maximum(largest, LEAST)))
    scaled = value * (TOP * jnp.exp2(-exponent))
    power = scaled
    for _ in range(POWER.bit_length() - 1):
        power = power * power
    out_ref[:rows, :] = (power * scaled).astype(out_ref.dtype)
    out_ref[rows:, :] = jnp.broadcast_to(exponent, (SPARE, width)).astype(out_ref.dtype)


def read_coded(ref):
    rows = ref.shape[0] - SPARE
    power = ref[:rows, :].astype(jnp.float32)
    exponent = ref[rows:, :].astype(jnp.float32)[:1, :]
    size = jnp.exp2(jnp.log2(jnp.maximum(jnp.abs(power), SMALLEST)) * (1.0 / POWER))
    size = jnp.where(power < 0, -size, size) * (jnp.exp2(exponent) * (1.0 / TOP))
    return jnp.where(power == 0, 0.0, size)


def second_kernel(pair_ref, out_ref):
    out_ref[...] = pair_ref[1:]


def multiply_kernel(spots, out_count, w_ref, choice_ref, *refs):
    out_refs = refs[-out_count:]
    blocks = [refs[n][spot] for n, spot in spots]
    tiles = choice_ref.shape[0]
    each = tiles // out_count
    for n, out_ref in enumerate(out_refs):
        products = []
        for tile in range(n * each, (n + 1) * each):
            left = jnp.zeros_like(blocks[0])
            for spot, block in enumerate(blocks):
                left = jnp.where(choice_ref[tile, spot : spot + 1, :] > 0.5, block, left)
            products.append(
                lax.dot_general(
                    left,
                    w_ref[:, tile * TILE : (tile + 1) * TILE],
                    (((0,), (0,)), ((), ())),
                    preferred_element_type=jnp.float32,
                )
            )
        value = jnp.concatenate(products, axis=1)
        if out_ref.dtype == jnp.float32:
            out_ref[...] = value
        else:
            write_coded(out_ref, value)


def scale_kernel(
    a_width, i_hbm, j_hbm, tile_hbm, ei_hbm, ej_hbm, ev_ref, after_hbm, inverse_ref, run_ref,
    zero_hbm, i_ref, j_ref, tile_ref, ei_ref, ej_ref, column_ref, zero_ref, sems, zero_sems,
):
    copies = start_all(
        (i_hbm, j_hbm, tile_hbm, ei_hbm, ej_hbm), (i_ref, j_ref, tile_ref, ei_ref, ej_ref), sems
    )
    rows_i, b_width = i_ref.shape[0], run_ref.shape[1]
    run = rows_i // tile_ref.shape[0]
    zero_ref[...] = jnp.zeros_like(zero_ref)
    count = zero_ref.shape[0]
    zero_copies = start_all(
        [zero_ref] * (rows_i // count),
        [zero_hbm.at[pl.ds(n * count, count)] for n in range(rows_i // count)],
        zero_sems,
    )
    a_start = lax.axis_index("blk") * a_width
    b_start = lax.axis_index("rep") * b_width
    a_tile = a_start // TILE
    column_ref[...] = jnp.broadcast_to(ev_ref[pl.ds(a_tile, 1), :], (TILE, TILE)).T
    a_energy = column_ref[pl.ds(pl.multiple_of(a_start % TILE, a_width), a_width), :]
    width = min(TILE, b_width)
    for copy in copies:
        copy.wait()
    for part in range(b_width // width):
        b_tile = b_start // TILE + part
        b_tile_row = ev_ref[pl.ds(b_tile, 1), :]
        b_row = b_tile_row[:, :width]
        for n in range(1, TILE // width):
            piece = b_tile_row[:, n * width : (n + 1) * width]
            b_row = jnp.where(b_start % TILE == n * width, piece, b_row)
        chosen = place_of(i_ref, run, j_ref[0] ^ tile_ref[a_tile] ^ tile_ref[b_tile])
        columns = slice(part * width, (part + 1) * width)
        run_ref[:, columns] = jnp.full((run_ref.shape[0], width), chosen.astype(jnp.float32))
        sum_ab = a_energy[:, :width] + b_row
        for m in range(run):
            inverse_ref[m * a_width : (m + 1) * a_width, columns] = 1.0 / (
                sum_ab - ei_ref[chosen * run + m] - ej_ref[0]
            )
    for copy in zero_copies:
        copy.wait()


def add_kernel(part_ref, so_far_ref, out_ref):
    out_ref[...] = so_far_ref[...] + read_coded(part_ref)


def place_kernel(run, inverse_ref, run_ref, zero_hbm, *refs):
    parts_refs, out_hbm, block_ref, sems = refs[:-3], refs[-3], refs[-2], refs[-1]
    a_width, width = block_ref.shape[2:]
    spans = [slice(n * width, (n + 1) * width) for n in range(block_ref.shape[0])]
    chosen_runs = [jnp.max(run_ref[:, columns]).astype(jnp.int32) for columns in spans]
    total = parts_refs[-1][...]
    for parts_ref in parts_refs[:-1]:
        coded = parts_ref.dtype != jnp.float32
        total = total + (read_coded(parts_ref) if coded else parts_ref[...])
    scaled = total * inverse_ref[...]
    copies = []
    for part, (columns, chosen) in enumerate(zip(spans, chosen_runs)):
        for m in range(run):
            block_ref[part, m] = scaled[m * a_width : (m + 1) * a_width, columns]
        target = out_hbm.at[pl.ds(chosen * run, run), :, pl.ds(part * width, width)]
        copies.append(pltpu.make_async_copy(block_ref.at[part], target, sems.at[part]))
        copies[-1].start()
    for copy in copies:
        copy.wait()


def swap(block, axis, step):
    return lax.ppermute(block, axis, [(n, n ^ step) for n in range(lax.axis_size(axis))])


def shards(t_slab, w_cycle, k_irrep, i_irrep, j_irrep, tile_irrep, i_energy, j_energy, vir_energy):
    blk_count = lax.axis_size("blk")
    rep_count = lax.axis_size("rep")
    k_rows, c_width, rows_i, full_width = t_slab.shape
    rows_j = w_cycle.shape[1]
    assert k_rows == 1 and rows_j == 1
    tiles = tile_irrep.shape[0]
    run = rows_i // tiles
    a_width = full_width // blk_count
    b_width = full_width // rep_count
    deep = c_width * run
    wide = run * a_width
    by_partner = a_width == TILE and b_width % TILE == 0 and run == 1
    steps = list(reversed(range(tiles))) if by_partner else list(range(tiles))
    groups = [[step] for step in steps]
    if by_partner:
        far = [4, 6, 2] if tiles == 8 else range(tiles - 2, 0, -2)
        groups = [[step, step + 1] for step in far] + [[1], [0]]
        steps = [step for group in groups for step in group]

    t_rows = t_slab.reshape(c_width * rows_i, full_width)

    def pack(some_groups, last):
        pairs = sum(len(group) for group in some_groups) // 2
        plan = (rows_i, run, c_width, by_partner, b_width // TILE, some_groups, steps * last)
        arguments = [k_irrep, i_irrep, tile_irrep, t_rows]
        shapes = [
            jax.ShapeDtypeStruct((len(group), deep, TILE), t_slab.dtype) for group in some_groups
        ]
        scratch = [
            small(k_irrep),
            small(i_irrep),
            small(tile_irrep),
            pltpu.VMEM((pairs, t_rows.shape[0], 2 * TILE), t_slab.dtype),
            pltpu.SemaphoreType.DMA((3 + last,)),
            pltpu.SemaphoreType.DMA((pairs,)),
        ]
        if last:
            arguments += [j_irrep, w_cycle.reshape(full_width, full_width)]
            shapes += [
                jax.ShapeDtypeStruct((TILE, full_width), w_cycle.dtype),
                jax.ShapeDtypeStruct((tiles, tiles, TILE), jnp.float32),
            ]
            scratch += [small(j_irrep), pltpu.SemaphoreType.DMA((tiles,))]
        return pl.pallas_call(
            lambda *refs: pack_kernel(plan, *refs),
            in_specs=[hbm()] * len(arguments),
            out_specs=[vmem()] * len(shapes),
            out_shape=shapes,
            scratch_shapes=scratch,
            compiler_params=limit(52 if last else 62),
            name="pack_near" if last else "pack_far",
        )(*arguments)

    packed = list(pack(groups[:3], False)) if by_partner else []
    *near, chosen_w, choice = pack(groups[len(packed) :], True)
    packed += near

    if by_partner:
        *far, beside, own = packed
        left = [swap(pair, "blk", group[0]) for pair, group in zip(far, groups)]
        left += [swap(beside, "blk", 1), own]
        left[2], left[-2], choice = lax.optimization_barrier((left[2], left[-2], choice))
        handed = []
        for pair in left[: len(far)]:
            block = pl.pallas_call(
                second_kernel,
                in_specs=[vmem()],
                out_specs=vmem(),
                out_shape=jax.ShapeDtypeStruct((1,) + pair.shape[1:], pair.dtype),
                compiler_params=limit(8),
                name="second",
            )(pair)
            handed.append(swap(block, "blk", 1))
        spots = []
        for n in range(len(far)):
            spots += [(n, 0), (len(left) + n, 0)]
        spots += [(len(far), 0), (len(far) + 1, 0)]
        left += handed
        part_shapes = [
            jax.ShapeDtypeStruct((wide + SPARE, b_width), jnp.bfloat16)
        ] * (rep_count - 1) + [jax.ShapeDtypeStruct((wide, b_width), jnp.float32)]
    else:
        stacked = jnp.concatenate(packed).reshape(tiles, c_width, run, TILE // a_width, a_width)
        outgoing = stacked.transpose(0, 3, 1, 2, 4).reshape(blk_count, c_width, wide)
        arrived = lax.all_to_all(outgoing, "blk", split_axis=0, concat_axis=0, tiled=True)
        left = [arrived.reshape(tiles, TILE, wide)]
        spots = [(0, n) for n in range(tiles)]
        part_shapes = [jax.ShapeDtypeStruct((wide, full_width), jnp.float32)]

    partials = pl.pallas_call(
        lambda *refs: multiply_kernel(spots, len(part_shapes), *refs),
        in_specs=[vmem()] * (2 + len(left)),
        out_specs=[vmem()] * len(part_shapes),
        out_shape=part_shapes,
        compiler_params=limit(16),
        name="multiply",
    )(chosen_w, choice, *left)

    out_shape = jax.ShapeDtypeStruct((rows_i, a_width, b_width), jnp.float32)
    inverse, run_row, zeros = pl.pallas_call(
        lambda *refs: scale_kernel(a_width, *refs),
        in_specs=[hbm()] * 5 + [vmem(), pl.BlockSpec(memory_space=pl.ANY)],
        out_specs=[vmem(), vmem(), hbm()],
        out_shape=[
            jax.ShapeDtypeStruct((wide, b_width), jnp.float32),
            jax.ShapeDtypeStruct((8, b_width), jnp.float32),
            out_shape,
        ],
        scratch_shapes=[
            small(i_irrep),
            small(j_irrep),
            small(tile_irrep),
            small(i_energy),
            small(j_energy),
            pltpu.VMEM((TILE, TILE), jnp.float32),
            pltpu.VMEM((run, a_width, b_width), jnp.float32),
            pltpu.SemaphoreType.DMA((5,)),
            pltpu.SemaphoreType.DMA((tiles,)),
        ],
        compiler_params=limit(8),
        name="scale",
    )(
        i_irrep, j_irrep, tile_irrep, i_energy, j_energy,
        vir_energy.reshape(full_width // TILE, TILE), partials[-1],
    )

    if by_partner:
        gathered = [
            swap(part, "rep", rep_count - 1 - n) for n, part in enumerate(partials[:-1])
        ] + [partials[-1]]
        while len(gathered) > 2:
            first, *gathered, so_far = gathered
            added = pl.pallas_call(
                add_kernel,
                in_specs=[vmem()] * 2,
                out_specs=vmem(),
                out_shape=jax.ShapeDtypeStruct(so_far.shape, so_far.dtype),
                compiler_params=limit(8),
                name="add",
            )(first, so_far)
            gathered.append(added)
    else:
        outgoing = partials[0].reshape(wide, rep_count, b_width).transpose(1, 0, 2)
        arrived = lax.all_to_all(outgoing, "rep", split_axis=0, concat_axis=0, tiled=True)
        gathered = [arrived[n] for n in range(rep_count)]

    part_width = min(TILE, b_width)
    result = pl.pallas_call(
        lambda *refs: place_kernel(run, *refs),
        in_specs=[vmem(), vmem(), hbm()] + [vmem()] * len(gathered),
        out_specs=hbm(),
        out_shape=out_shape,
        input_output_aliases={2: 0},
        scratch_shapes=[
            pltpu.VMEM((b_width // part_width, run, a_width, part_width), jnp.float32),
            pltpu.SemaphoreType.DMA((b_width // part_width,)),
        ],
        compiler_params=limit(16),
        name="place",
    )(inverse, run_row, zeros, *gathered)
    return result.reshape(rows_j, rows_i, a_width, b_width)


def solution(mesh):
    in_specs = (
        P("rep", "blk", None, None),
        P("rep", None, None, None),
        P("rep"),
        P(),
        P(),
        P(),
        P(),
        P(),
        P(),
    )
    out_specs = P(None, None, "blk", "rep")
    return jax.shard_map(shards, mesh=mesh, in_specs=in_specs, out_specs=out_specs, check_vma=False)
```
